256 devices in a mesh: beam: 8 (over x, core), row: 32 (over y, z).
Axes of the slice: x: 4, y: 4, z: 8, core: 2. Of those that a mesh axis runs over, the one named last changes fastest.
Arguments:
- dirty: float32 [8, 2048, 2048], P('beam', 'row'), may hold values from -6 to 6
- model: bfloat16 [8, 2048, 2048], P('beam', 'row'), may hold values from -6 to 6
- psf_spectrum: float32 [8, 2, 2048, 2048], P('beam', None, None, 'row'), may hold values from -4 to 4
- primary_beam: bfloat16 [8, 2048, 2048], P('beam', 'row'), may hold values from 0.049804688 to 1
- offsets: int32 [8], replicated, may hold values from 0 to 16
Outputs:
- residual: float32 [8, 2048, 2048], P('beam', 'row')
- returned: float32 [8, 2048, 2048], P('beam', 'row')
The draws below stay inside these ranges and needn't reach their ends.
All inputs are finite; a program needn't handle non-finite values.
Results may differ from the reference program's by a relative error of at most 0.013.
Values may be sent and summed in bfloat16 or wider, within the bound.
A program may use at most 64 MiB of HBM per device.

```python
import math
import jax
import jax.numpy as jnp
from jax import lax

N = 2048
PA = 32
BW = 128
BEAMS = 8
NC = 16
TILES = 32


def with_ends(drawn, rng, low, high):
    longest = drawn.shape.index(max(drawn.shape))
    spots = []
    for shift in (0, 1):
        where = [jax.random.randint(jax.random.fold_in(rng, axis), (), 0, length) for axis, length in enumerate(drawn.shape)]
        where[longest] = (where[longest] + shift) % drawn.shape[longest]
        spots.append(tuple(where))
    return drawn.at[spots[0]].set(low).at[spots[1]].set(high)


def steps_of(key, shape, cuts, smallest, largest):
    loudness, own = 1.0, jax.random.fold_in(key, 6)
    for dim, shards_of in cuts:
        heights = jnp.exp(jax.random.uniform(jax.random.fold_in(own, dim), (shards_of,), jnp.float32, smallest / len(cuts), largest / len(cuts)))
        loudness = loudness * jnp.repeat(heights, shape[dim] // shards_of).reshape([-1 if axis == dim else 1 for axis in range(len(shape))])
    return loudness


def noise(own_key, extent, deviation, limit, cuts=(), held_as=jnp.bfloat16):
    gain = steps_of(own_key, extent, cuts, -0.22, 0.18) if cuts else 1.0
    entries = jax.random.normal(own_key, extent, jnp.float32) * deviation * gain
    return jnp.minimum(jnp.maximum(entries, -limit), limit).astype(held_as)


def setup_inputs(seed: int = 0) -> dict:
    splits = jax.random.split(jax.random.key(seed), 6)
    dirty = noise(splits[0], (BEAMS, N, N), 1.0, 6.0, ((0, 8), (1, 32)), jnp.float32)
    model = noise(splits[1], (BEAMS, N, N), 1.0, 6.0, ((0, 8), (1, 32)))
    psf_spectrum = noise(splits[2], (BEAMS, 2, N, N), 0.7, 4.0, ((0, 8), (3, 32)), jnp.float32)
    primary_beam = jnp.clip(jnp.exp(math.log(1.0) - 2.9996462 * jax.random.uniform(splits[3], (BEAMS, N, N), jnp.float32) ** steps_of(splits[3], (BEAMS, N, N), ((0, 8), (1, 32)), -0.2, 0.2)), 0.049804688, 1.0).astype(jnp.bfloat16)
    offsets = with_ends(jax.random.randint(splits[4], (BEAMS,), 0, NC + 1), jax.random.fold_in(splits[4], 1), 0, NC).astype(jnp.int32)
    return {"dirty": dirty, "model": model, "psf_spectrum": psf_spectrum, "primary_beam": primary_beam, "offsets": offsets}


weight_floor = 0.05

def phase_pair(count, other, modulus, sign):
    left = jnp.arange(count, dtype=jnp.int32)
    right = jnp.arange(other, dtype=jnp.int32)
    phase = (left[:, None] * right[None, :] % modulus).astype(jnp.float32) * (2.0 * math.pi / modulus)
    return (jnp.cos(phase), sign * jnp.sin(phase))

def make_tables(size, first, sign):
    second = size // first
    cos_one, sin_one = phase_pair(first, first, first, sign)
    scale_one = 1.0 / math.sqrt(first)
    cos_one = (cos_one * scale_one).astype(jnp.bfloat16)
    sin_one = (sin_one * scale_one).astype(jnp.bfloat16)
    twid_cos, twid_sin = phase_pair(first, second, size, sign)
    cos_two, sin_two = phase_pair(second, second, second, sign)
    scale_two = 1.0 / math.sqrt(second)
    return (cos_one, sin_one, twid_cos, twid_sin, cos_two * scale_two, sin_two * scale_two)

def exact(spec, left, right):
    return jnp.einsum(spec, left.astype(jnp.float32), right.astype(jnp.float32), precision=lax.Precision.HIGHEST, preferred_element_type=jnp.float32)

def transform(real_in, imag_in, tables, along_rows, real_only):
    cos_one, sin_one, twid_cos, twid_sin, cos_two, sin_two = tables
    first = cos_one.shape[0]
    second = cos_two.shape[0]
    shape = real_in.shape
    if along_rows:
        split = (shape[0], first, second, shape[2])
        spec_one = 'bpql,pk->bkql'
        spec_two = 'bkql,qm->bmkl'
        twid_cos = twid_cos[:, :, None]
        twid_sin = twid_sin[:, :, None]
    else:
        split = (shape[0], shape[1], first, second)
        spec_one = 'brpq,pk->brkq'
        spec_two = 'brkq,qm->brmk'
    real_x = real_in.reshape(split)
    part_real = exact(spec_one, real_x, cos_one)
    part_imag = exact(spec_one, real_x, sin_one)
    if imag_in is not None:
        imag_x = imag_in.reshape(split)
        part_real = part_real - exact(spec_one, imag_x, sin_one)
        part_imag = part_imag + exact(spec_one, imag_x, cos_one)
    turned_real = part_real * twid_cos - part_imag * twid_sin
    turned_imag = part_imag * twid_cos + part_real * twid_sin
    out_real = exact(spec_two, turned_real, cos_two) - exact(spec_two, turned_imag, sin_two)
    if real_only:
        return out_real.reshape(shape)
    out_imag = exact(spec_two, turned_imag, cos_two) + exact(spec_two, turned_real, sin_two)
    return (out_real.reshape(shape), out_imag.reshape(shape))

def reference(dirty, model, psf_spectrum, primary_beam, offsets):
    forward = make_tables(N, PA, -1)
    inverse = make_tables(N, PA, 1)

    def one_beam(items):
        image, spectrum, dirty_one = items
        f1_real, f1_imag = transform(image[None], None, forward, False, False)
        f1_real = f1_real.astype(jnp.bfloat16)
        f1_imag = f1_imag.astype(jnp.bfloat16)
        freq_real, freq_imag = transform(f1_real, f1_imag, forward, True, False)
        h_real = (freq_real * spectrum[0] - freq_imag * spectrum[1]).astype(jnp.bfloat16)
        h_imag = (freq_real * spectrum[1] + freq_imag * spectrum[0]).astype(jnp.bfloat16)
        g_real, g_imag = transform(h_real, h_imag, inverse, True, False)
        g_real = g_real.astype(jnp.bfloat16)
        g_imag = g_imag.astype(jnp.bfloat16)
        convolved = transform(g_real, g_imag, inverse, False, True)
        return dirty_one - convolved[0]
    residual = lax.map(one_beam, (model, psf_spectrum, dirty))
    beam_f = primary_beam.astype(jnp.float32)
    weighted = (beam_f * residual).astype(jnp.bfloat16)
    blocks = weighted.astype(jnp.float32).reshape(BEAMS, N, NC, BW)
    squares = (beam_f * beam_f).reshape(BEAMS, N, NC, BW)
    tile_of = offsets[:, None] + jnp.arange(NC, dtype=jnp.int32)[None, :]
    hits = (tile_of[:, :, None] == jnp.arange(TILES, dtype=jnp.int32)[None, None, :]).astype(jnp.float32)
    numer = jnp.einsum('bicw,bct->itw', blocks, hits)
    denom = jnp.einsum('bicw,bct->itw', squares, hits)
    joint_image = (numer / jnp.maximum(denom, weight_floor)).astype(jnp.bfloat16)
    looked = jnp.einsum('itw,bct->bicw', joint_image.astype(jnp.float32), hits).reshape(BEAMS, N, N)
    return (residual, beam_f * looked)
```

```python
import math

import jax
import jax.numpy as jnp
import numpy as np
from jax import lax
from jax.experimental import pallas as pl
from jax.experimental.pallas import tpu as pltpu
from jax.sharding import PartitionSpec as P

MESH = pl.DeviceIdType.MESH
F32 = jnp.float32
BF16 = jnp.bfloat16

N = 2048
ROWS = 64
NR = 32
NB = 8
NCH = 2
TPC = 4 // NCH
FLOOR = 0.05
RT = math.sqrt(0.5)


def place(a):
    return 8 * (a % 4) + a // 4


def tables():
    q = np.arange(256)
    k1 = np.arange(8)
    th = 2 * np.pi * (q[None, :] * k1[:, None] % 2048) / 2048
    tw1 = np.stack([np.cos(th), -np.sin(th)]) / math.sqrt(8.0)
    th = 2 * np.pi * (q[:, None] * q[None, :] % 256) / 256
    cos, sin = np.cos(th) / 16, np.sin(th) / 16
    w1 = np.empty((32, 2, 8, 2, 256))
    c3, s3 = cos.reshape(32, 8, 256), sin.reshape(32, 8, 256)
    w1[:, 0, :, 0], w1[:, 0, :, 1] = c3, s3
    w1[:, 1, :, 0], w1[:, 1, :, 1] = -s3, c3
    w4 = np.empty((32, 2, 8, 2, 256))
    w4[:, 0, :, 0], w4[:, 0, :, 1] = c3, s3
    w4[:, 1, :, 0], w4[:, 1, :, 1] = -s3, c3
    r = np.arange(64)
    th = 2 * np.pi * (r[:, None] * r[None, :] % 64) / 64
    cos, sin = np.cos(th) / 8, np.sin(th) / 8
    w2 = np.zeros((2, 2, 64, 2, 2, 64))
    w3 = np.zeros((2, 2, 64, 2, 2, 64))
    for x in range(2):
        w2[0, x, :, 0, x], w2[0, x, :, 1, x] = cos, -sin
        w2[1, x, :, 0, x], w2[1, x, :, 1, x] = sin, cos
        w3[0, x, :, 0, x], w3[0, x, :, 1, x] = cos, sin
        w3[1, x, :, 0, x], w3[1, x, :, 1, x] = -sin, cos
    a = np.arange(32)
    th = 2 * np.pi * (r[None, :] * a[:, None] % 2048) / 2048
    tw2 = np.empty((2, 32, 128))
    where = place(a)
    tw2[0, where] = np.tile(np.cos(th), (1, 2)) / math.sqrt(32.0)
    tw2[1, where] = np.tile(-np.sin(th), (1, 2)) / math.sqrt(32.0)
    p1 = np.zeros((256, 256))
    for m in range(8):
        p1[where * 8 + m, 32 * m + a] = 1
    p2 = np.zeros((2, 2, 4, 8, 2, 64))
    for c in range(2):
        for x in range(2):
            for t in range(4):
                for k in range(8):
                    p2[c, x, t, k, c, t + 4 * x + 8 * k] = 1
    bf = lambda v, *s: np.asarray(v.reshape(s), jnp.bfloat16)
    return (
        bf(w1, 512, 512),
        bf(w2, 256, 256),
        bf(w3, 256, 256),
        bf(w4, 512, 512),
        bf(p1, 256, 256),
        bf(p2, 128, 128),
        np.asarray(tw1, np.float32),
        np.asarray(tw2, np.float32),
    )


def add(x, y):
    return (x[0] + y[0], x[1] + y[1])


def sub(x, y):
    return (x[0] - y[0], x[1] - y[1])


def turn(x, s):
    return (-x[1], x[0]) if s > 0 else (x[1], -x[0])


def mul(x, c, d):
    return (x[0] * c - x[1] * d, x[0] * d + x[1] * c)


def mul_const(x, num, den, s):
    num %= den
    if num == 0:
        return x
    if 4 * num == den:
        return turn(x, s)
    if 2 * num == den:
        return (-x[0], -x[1])
    if 8 * num == den:
        r = F32(RT)
        return ((x[0] - s * x[1]) * r, (x[1] + s * x[0]) * r)
    if 8 * num == 3 * den:
        r = F32(RT)
        return ((-x[0] - s * x[1]) * r, (s * x[0] - x[1]) * r)
    th = 2 * math.pi * num / den
    return mul(x, F32(math.cos(th)), F32(s * math.sin(th)))


def dft4(x, s):
    t0, t1, t2, t3 = add(x[0], x[2]), sub(x[0], x[2]), add(x[1], x[3]), turn(sub(x[1], x[3]), s)
    return [add(t0, t2), add(t1, t3), sub(t0, t2), sub(t1, t3)]


def dft8(x, s):
    e, o = dft4(x[0::2], s), dft4(x[1::2], s)
    o = [mul_const(o[k], k, 8, s) for k in range(4)]
    return [add(e[k], o[k]) for k in range(4)] + [sub(e[k], o[k]) for k in range(4)]


def dft32_forward(x):
    cols = [dft4([x[8 * p1 + p0] for p1 in range(4)], -1) for p0 in range(8)]
    out = []
    for a0 in range(4):
        out += dft8([mul_const(cols[p0][a0], p0 * a0, 32, -1) for p0 in range(8)], -1)
    return out


def dft32_inverse(x):
    rows = [dft8(x[8 * a0 : 8 * a0 + 8], 1) for a0 in range(4)]
    out = [None] * 32
    for p0 in range(8):
        y = dft4([mul_const(rows[a0][p0], p0 * a0, 32, 1) for a0 in range(4)], 1)
        for p1 in range(4):
            out[8 * p1 + p0] = y[p1]
    return out


def dot(x, y, dims):
    return lax.dot_general(x, y, (dims, ((), ())), preferred_element_type=F32)


NN = ((1,), (0,))
NT = ((1,), (1,))


def kernel(
    model, dirty, pb, psf, offs, w1h, w2h, w3h, w4h, p1h, p2h, tw1h, tw2h,
    res_out, ret_out,
    model_v, dirty_v, pb_v, psf_v, w1, w2, w3, w4, p1, p2, tw1, tw2,
    z1, send1, recv1, send2, recv2, psfp, y_v, u_v, z2,
    pbf, sendw, recvw, send3, recv3, send4, recv4, buf, rden, joint, res_v, ret_v,
    lsem, osem, ssem, rsem,
):
    bme = lax.axis_index("beam")
    rme = lax.axis_index("row")
    yme, zme = rme // 8, rme % 8

    def row_peer(i):
        n = i // 4
        dz = 4 + (1 - 2 * (n % 2)) * ((n + 1) // 2)
        dy = 3 - i % 4
        return ((yme + dy) % 4) * 8 + (zme + dz) % 8

    def beam_peer(i):
        return (bme + 1 + i) % NB

    loads = [
        (model, model_v), (w1h, w1), (tw1h, tw1), (pb, pb_v), (psf, psf_v), (p1h, p1), (p2h, p2),
        (w2h, w2), (w3h, w3), (tw2h, tw2), (w4h, w4), (dirty, dirty_v),
    ]
    copies = [pltpu.make_async_copy(h, v, lsem.at[i]) for i, (h, v) in enumerate(loads)]
    for c in copies:
        c.start()

    barrier = pltpu.get_barrier_semaphore()

    def greet_row(i, _):
        pl.semaphore_signal(barrier, inc=1, device_id=(bme, row_peer(i)), device_id_type=MESH)
        return 0

    def greet_beam(i, _):
        pl.semaphore_signal(barrier, inc=1, device_id=(beam_peer(i), rme), device_id_type=MESH)
        return 0

    lax.fori_loop(0, NR - 1, greet_row, 0)
    lax.fori_loop(0, NB - 1, greet_beam, 0)

    copies[0].wait()
    copies[1].wait()
    copies[2].wait()
    for rb in range(4):
        for qt in range(2):
            rows = pl.ds(16 * rb, 16)
            x = [model_v[rows, pl.ds(256 * p + 128 * qt, 128)].astype(F32) for p in range(8)]
            a, b, c, d = x[1] - x[5], x[3] - x[7], x[0] - x[4], x[2] - x[6]
            s04, s26, s15, s37 = x[0] + x[4], x[2] + x[6], x[1] + x[5], x[3] + x[7]
            e0, o0 = s04 + s26, s15 + s37
            u, v = (a - b) * F32(RT), (a + b) * F32(RT)
            y1, y2, y3 = (c + u, -d - v), (s04 - s26, s37 - s15), (c - u, d - v)
            y = [(e0 + o0, None), y1, y2, y3, (e0 - o0, None), (y3[0], -y3[1]), (y2[0], -y2[1]), (y1[0], -y1[1])]
            for k in range(8):
                tc = tw1[0, pl.ds(k, 1), pl.ds(128 * qt, 128)]
                ts = tw1[1, pl.ds(k, 1), pl.ds(128 * qt, 128)]
                re, im = y[k]
                if im is None:
                    zr, zi = re * tc, re * ts
                else:
                    zr, zi = re * tc - im * ts, re * ts + im * tc
                to = pl.ds(64 * (k // 4) + 16 * rb, 16)
                z1[k % 4, to, pl.ds(128 * qt, 128)] = zr.astype(BF16)
                z1[k % 4, to, pl.ds(256 + 128 * qt, 128)] = zi.astype(BF16)

    def send_rows(phase, ch, src, dst):
        def go(i, _):
            peer = row_peer(i)
            pltpu.make_async_remote_copy(
                src_ref=src.at[ch, peer],
                dst_ref=dst.at[ch, rme],
                send_sem=ssem.at[phase * NCH + ch],
                recv_sem=rsem.at[phase * NCH + ch],
                device_id=(bme, peer),
                device_id_type=MESH,
            ).start()
            return 0

        lax.fori_loop(0, NR - 1, go, 0)
        dst[ch, rme] = src[ch, rme]

    def wait_rows(sems, phase, ch, dst):
        part = dst.at[ch, pl.ds(0, NR - 1)]
        pltpu.make_async_copy(part, part, sems.at[phase * NCH + ch]).wait()

    base = 2 * NCH

    def send_beam(which, peer, src, dst):
        pltpu.make_async_remote_copy(
            src_ref=src.at[peer],
            dst_ref=dst.at[bme],
            send_sem=ssem.at[base + which],
            recv_sem=rsem.at[base + which],
            device_id=(peer, rme),
            device_id_type=MESH,
        ).start()

    def wait_beam(sems, which, dst):
        part = dst.at[pl.ds(0, NB - 1)]
        pltpu.make_async_copy(part, part, sems.at[base + which]).wait()

    for ch in range(NCH):
        for i in range(TPC):
            t = ch * TPC + i
            out = dot(w1[...], z1[t], NT).astype(BF16)
            send1[ch, :, i] = out.reshape(NR, 16, 128)
        if ch == 0:
            pl.semaphore_wait(barrier, NR - 1 + NB - 1)
        send_rows(0, ch, send1, recv1)

    copies[3].wait()
    for rb in range(4):
        both = pb_v[pl.ds(16 * rb, 16), :].astype(F32)
        pbf[pl.ds(16 * rb, 16), :] = both
        for j in range(2):
            part = both[8 * j : 8 * j + 8]
            sendw[2 * rb + j] = jnp.concatenate([part[:, :1024], part[:, 1024:]], axis=0).astype(BF16)

    def go_w(i, _):
        send_beam(0, beam_peer(i), sendw, recvw)
        return 0

    lax.fori_loop(0, NB - 1, go_w, 0)
    recvw[bme] = sendw[bme]

    copies[4].wait()
    copies[5].wait()
    copies[6].wait()
    for m in range(8):
        part = psf_v[:, pl.ds(256 * m, 256)].astype(BF16)
        y_v[:, pl.ds(8 * m, 8), :] = dot(p1[...], part, NT).reshape(32, 8, 128)
    low = lax.broadcasted_iota(jnp.int32, (32, 128), 1) < 64
    for a in range(0, 32, 2):
        pair = y_v[pl.ds(a, 2)].reshape(128, 128).astype(BF16)
        got = dot(p2[...], pair, NT)
        for c in range(2):
            one, two = got[64 * c : 64 * c + 32], got[64 * c + 32 : 64 * c + 64]
            first = jnp.where(low, one, pltpu.roll(two, 64, 1))
            second = jnp.where(low, pltpu.roll(one, 64, 1), two)
            for t in range(4):
                psfp[t, c, pl.ds(8 * a, 8), :] = first[8 * t : 8 * t + 8]
                psfp[t, c, pl.ds(8 * a + 8, 8), :] = second[8 * t : 8 * t + 8]

    for b in range(NB):
        buf[b, pl.ds(0, 16)] = jnp.zeros((16, 8, 128), F32)
        buf[b, pl.ds(32, 16)] = jnp.zeros((16, 8, 128), F32)

    copies[7].wait()
    copies[8].wait()
    copies[9].wait()

    for ch in range(NCH):
        wait_rows(rsem, 0, ch, recv1)
        for i in range(TPC):
            t = ch * TPC + i
            x = []
            for p in range(NR):
                both = recv1[ch, p, i].astype(F32)
                x.append((both[:8], both[8:]))
            x = dft32_forward(x)
            for a in range(0, NR, 2):
                turned = [mul(x[a + j], tw2[0, pl.ds(a + j, 1), :], tw2[1, pl.ds(a + j, 1), :]) for j in range(2)]
                for c in range(2):
                    z2[pl.ds(8 * a, 16), pl.ds(128 * c, 128)] = jnp.concatenate(
                        [turned[0][c], turned[1][c]], axis=0
                    ).astype(BF16)
            f = dot(z2[...], w2[...], NN)
            fr, fi = f[:, :128], f[:, 128:]
            pr, pi = psfp[t, 0], psfp[t, 1]
            h = jnp.concatenate([(fr * pr - fi * pi).astype(BF16), (fr * pi + fi * pr).astype(BF16)], axis=1)
            g = dot(h, w3[...], NN)
            x = []
            for a in range(NR):
                gr, gi = g[8 * a : 8 * a + 8, :128], g[8 * a : 8 * a + 8, 128:]
                x.append(mul((gr, gi), tw2[0, pl.ds(a, 1), :], -tw2[1, pl.ds(a, 1), :]))
            x = dft32_inverse(x)
            for p in range(NR):
                send2[ch, p, i] = jnp.concatenate([x[p][0], x[p][1]], axis=0).astype(BF16)
        send_rows(1, ch, send2, recv2)

    def tile_sum(t):
        total = None
        for b in range(NB):
            one = buf[b, t - offs[b] + 16]
            total = one if total is None else total + one
        return total

    wait_beam(rsem, 0, recvw)
    for b in range(NB):
        for c in range(8):
            both = recvw[b, :, pl.ds(128 * c, 128)].astype(F32)
            both = both * both
            buf[b, 16 + c] = both[:8]
            buf[b, 24 + c] = both[8:]

    def weigh(t, _):
        rden[t] = 1.0 / jnp.maximum(tile_sum(t), FLOOR)
        return 0

    lax.fori_loop(0, 32, weigh, 0)

    copies[10].wait()
    for ch in range(NCH):
        wait_rows(rsem, 1, ch, recv2)
        for i in range(TPC):
            t = ch * TPC + i
            got = recv2[ch, :, i].reshape(512, 128)
            u_v[t] = dot(got.T, w4[...], NN)

    copies[11].wait()

    def last(i, _):
        rb = beam_peer(i)
        row0 = pl.multiple_of(8 * rb, 8)
        rows = pl.ds(row0, 8)
        for qt in range(2):
            v = []
            for k in range(8):
                at = pl.ds(pl.multiple_of(64 * (k // 4) + 8 * rb, 8), 8)
                ur = u_v[k % 4, at, pl.ds(128 * qt, 128)]
                ui = u_v[k % 4, at, pl.ds(256 + 128 * qt, 128)]
                tc = tw1[0, pl.ds(k, 1), pl.ds(128 * qt, 128)]
                ts = -tw1[1, pl.ds(k, 1), pl.ds(128 * qt, 128)]
                re = ur * tc - ui * ts
                v.append((re, None if k % 4 == 0 else ur * ts + ui * tc))
            s = [None] + [(v[k][0] + v[8 - k][0], v[k][1] - v[8 - k][1]) for k in (1, 2, 3)]
            pp, mm = v[0][0] + v[4][0], v[0][0] - v[4][0]
            e1, e2 = pp + s[2][0], pp - s[2][0]
            o1, o2 = mm - s[2][1], mm + s[2][1]
            f, g = s[1][0] + s[3][0], s[1][1] - s[3][1]
            u = F32(RT) * ((s[1][0] - s[1][1]) - (s[3][0] + s[3][1]))
            w = F32(RT) * ((s[1][0] + s[1][1]) - (s[3][0] - s[3][1]))
            conv = [e1 + f, o1 + u, e2 - g, o2 - w, e1 - f, o1 - u, e2 + g, o2 + w]
            weighted = []
            for p in range(8):
                cols = pl.ds(256 * p + 128 * qt, 128)
                one = dirty_v[rows, cols] - conv[p]
                res_v[rows, cols] = one
                weighted.append(pbf[rows, cols] * one)
            for p in range(4):
                send3[rb, :, pl.ds(256 * p + 128 * qt, 128)] = jnp.concatenate(
                    [weighted[p], weighted[p + 4]], axis=0
                ).astype(BF16)

        @pl.when(i < NB - 1)
        def _():
            send_beam(1, rb, send3, recv3)

        return 0

    lax.fori_loop(0, NB, last, 0)
    recv3[bme] = send3[bme]
    res_copy = pltpu.make_async_copy(res_v, res_out, osem.at[0])
    res_copy.start()

    wait_beam(rsem, 1, recv3)
    for b in range(NB):
        for c in range(8):
            both = recv3[b, :, pl.ds(128 * c, 128)].astype(F32)
            buf[b, 16 + c] = both[:8]
            buf[b, 24 + c] = both[8:]

    def join(t, _):
        joint[t] = tile_sum(t) * rden[t]
        return 0

    lax.fori_loop(0, 32, join, 0)

    def reply(i, _):
        b = beam_peer(i)
        off = offs[b]
        for c in range(8):
            send4[b, :, pl.ds(128 * c, 128)] = jnp.concatenate([joint[off + c], joint[off + 8 + c]], axis=0).astype(BF16)

        @pl.when(i < NB - 1)
        def _():
            send_beam(2, b, send4, recv4)

        return 0

    lax.fori_loop(0, NB, reply, 0)
    recv4[bme] = send4[bme]
    wait_beam(rsem, 2, recv4)
    for b in range(NB):
        for h in range(2):
            rows, cols = pl.ds(8 * b, 8), pl.ds(1024 * h, 1024)
            looked = recv4[b].astype(F32)[8 * h : 8 * h + 8]
            ret_v[rows, cols] = pbf[rows, cols] * looked
    ret_copy = pltpu.make_async_copy(ret_v, ret_out, osem.at[1])
    ret_copy.start()

    for ch in range(NCH):
        wait_rows(ssem, 0, ch, recv1)
        wait_rows(ssem, 1, ch, recv2)
    wait_beam(ssem, 0, recvw)
    wait_beam(ssem, 1, recv3)
    wait_beam(ssem, 2, recv4)
    res_copy.wait()
    ret_copy.wait()


def body(dirty, model, psf_spectrum, primary_beam, offsets):
    consts = [jnp.asarray(v) for v in tables()]
    psf = jnp.swapaxes(psf_spectrum[0], 1, 2).reshape(128, N)
    hbm = pl.BlockSpec(memory_space=pl.ANY)
    image = lambda dt: pltpu.VMEM((ROWS, N), dt)
    block = lambda: pltpu.VMEM((NCH, NR, TPC, 16, 128), BF16)
    beam = lambda: pltpu.VMEM((NB, 16, 1024), BF16)
    scratch = [
        image(BF16), image(F32), image(BF16), pltpu.VMEM((128, N), F32),
        *[pltpu.VMEM(v.shape, v.dtype) for v in consts],
        pltpu.VMEM((4, 128, 512), BF16), block(), block(), block(), block(),
        pltpu.VMEM((4, 2, 256, 128), F32), pltpu.VMEM((32, 64, 128), F32), pltpu.VMEM((4, 128, 512), F32),
        pltpu.VMEM((256, 256), BF16),
        image(F32), beam(), beam(), beam(), beam(), beam(), beam(),
        pltpu.VMEM((NB, 48, 8, 128), F32), pltpu.VMEM((32, 8, 128), F32), pltpu.VMEM((32, 8, 128), F32),
        image(F32), image(F32),
        pltpu.SemaphoreType.DMA((12,)), pltpu.SemaphoreType.DMA((2,)),
        pltpu.SemaphoreType.DMA((2 * NCH + 3,)), pltpu.SemaphoreType.DMA((2 * NCH + 3,)),
    ]
    residual, returned = pl.pallas_call(
        kernel,
        out_shape=[jax.ShapeDtypeStruct((ROWS, N), F32)] * 2,
        in_specs=[hbm] * 4 + [pl.BlockSpec(memory_space=pltpu.SMEM)] + [hbm] * 8,
        out_specs=[hbm] * 2,
        scratch_shapes=scratch,
        compiler_params=pltpu.CompilerParams(
            collective_id=0, has_side_effects=True, vmem_limit_bytes=48 * 1024 * 1024
        ),
    )(model[0], dirty[0], primary_beam[0], psf, offsets, *consts)
    return (residual[None], returned[None])


def solution(mesh):
    in_specs = (
        P("beam", "row", None),
        P("beam", "row", None),
        P("beam", None, None, "row"),
        P("beam", "row", None),
        P(),
    )
    out_specs = (P("beam", "row", None), P("beam", "row", None))
    return jax.shard_map(body, mesh=mesh, in_specs=in_specs, out_specs=out_specs, check_vma=False)
```

```python
import math

import jax
import jax.numpy as jnp
import numpy as np
from jax import lax
from jax.experimental import pallas as pl
from jax.experimental.pallas import tpu as pltpu
from jax.sharding import PartitionSpec as P

MESH = pl.DeviceIdType.MESH
F32 = jnp.float32
BF16 = jnp.bfloat16

N = 2048
ROWS = 64
NR = 32
NB = 8
FIRST = (0, 2, 1, 3)
FLOOR = 0.05
RT = math.sqrt(0.5)


def place(a):
    return 8 * (a % 4) + a // 4


def tables():
    q = np.arange(256)
    k1 = np.arange(8)
    th = 2 * np.pi * (q[None, :] * k1[:, None] % 2048) / 2048
    tw1 = np.stack([np.cos(th), -np.sin(th)]) / math.sqrt(8.0)
    th = 2 * np.pi * (q[:, None] * q[None, :] % 256) / 256
    cos, sin = np.cos(th) / 16, np.sin(th) / 16
    w1 = np.empty((32, 2, 8, 2, 256))
    c3, s3 = cos.reshape(32, 8, 256), sin.reshape(32, 8, 256)
    w1[:, 0, :, 0], w1[:, 0, :, 1] = c3, s3
    w1[:, 1, :, 0], w1[:, 1, :, 1] = -s3, c3
    w4 = np.empty((32, 2, 8, 2, 256))
    w4[:, 0, :, 0], w4[:, 0, :, 1] = c3, s3
    w4[:, 1, :, 0], w4[:, 1, :, 1] = -s3, c3
    r = np.arange(64)
    th = 2 * np.pi * (r[:, None] * r[None, :] % 64) / 64
    cos, sin = np.cos(th) / 8, np.sin(th) / 8
    w2 = np.zeros((2, 2, 64, 2, 2, 64))
    w3 = np.zeros((2, 2, 2, 64, 2, 2, 2, 2, 32))
    for x in range(2):
        w2[0, x, :, 0, x], w2[0, x, :, 1, x] = cos, -sin
        w2[1, x, :, 0, x], w2[1, x, :, 1, x] = sin, cos
        for t in range(2):
            for hi in range(2):
                part = slice(32 * hi, 32 * hi + 32)
                w3[t, 0, x, :, hi, 0, t, x], w3[t, 0, x, :, hi, 1, t, x] = cos[:, part], sin[:, part]
                w3[t, 1, x, :, hi, 0, t, x], w3[t, 1, x, :, hi, 1, t, x] = -sin[:, part], cos[:, part]
    a = np.arange(32)
    th = 2 * np.pi * (r[None, :] * a[:, None] % 2048) / 2048
    tw2 = np.empty((2, 32, 128))
    where = place(a)
    tw2[0, where] = np.tile(np.cos(th), (1, 2)) / math.sqrt(32.0)
    tw2[1, where] = np.tile(-np.sin(th), (1, 2)) / math.sqrt(32.0)
    tw3 = np.empty((2, 2, 32, 128))
    for hi in range(2):
        part = th[:, 32 * hi : 32 * hi + 32]
        tw3[hi, 0, where] = np.tile(np.cos(part), (1, 4)) / math.sqrt(32.0)
        tw3[hi, 1, where] = np.tile(np.sin(part), (1, 4)) / math.sqrt(32.0)
    p1 = np.zeros((256, 256))
    for m in range(8):
        p1[where * 8 + m, 32 * m + a] = 1
    p2 = np.zeros((2, 2, 4, 8, 2, 64))
    for c in range(2):
        for x in range(2):
            for t in range(4):
                for k in range(8):
                    p2[c, x, t, k, c, FIRST[t] + 4 * x + 8 * k] = 1
    bf = lambda v, *s: np.asarray(v.reshape(s), jnp.bfloat16)
    return (
        bf(w1, 512, 512),
        bf(w2, 256, 256),
        bf(w3, 512, 512),
        bf(w4, 512, 512),
        bf(p1, 256, 256),
        bf(p2, 128, 128),
        np.asarray(tw1, np.float32),
        np.asarray(tw2, np.float32),
        np.asarray(tw3, np.float32),
    )


def add(x, y):
    return (x[0] + y[0], x[1] + y[1])


def sub(x, y):
    return (x[0] - y[0], x[1] - y[1])


def turn(x, s):
    return (-x[1], x[0]) if s > 0 else (x[1], -x[0])


def mul(x, c, d):
    return (x[0] * c - x[1] * d, x[0] * d + x[1] * c)


def mul_const(x, num, den, s):
    num %= den
    if num == 0:
        return x
    if 4 * num == den:
        return turn(x, s)
    if 2 * num == den:
        return (-x[0], -x[1])
    if 8 * num == den:
        r = F32(RT)
        return ((x[0] - s * x[1]) * r, (x[1] + s * x[0]) * r)
    if 8 * num == 3 * den:
        r = F32(RT)
        return ((-x[0] - s * x[1]) * r, (s * x[0] - x[1]) * r)
    th = 2 * math.pi * num / den
    return mul(x, F32(math.cos(th)), F32(s * math.sin(th)))


def dft4(x, s):
    t0, t1, t2, t3 = add(x[0], x[2]), sub(x[0], x[2]), add(x[1], x[3]), turn(sub(x[1], x[3]), s)
    return [add(t0, t2), add(t1, t3), sub(t0, t2), sub(t1, t3)]


def dft8(x, s):
    e, o = dft4(x[0::2], s), dft4(x[1::2], s)
    o = [mul_const(o[k], k, 8, s) for k in range(4)]
    return [add(e[k], o[k]) for k in range(4)] + [sub(e[k], o[k]) for k in range(4)]


def dft32_forward(x):
    cols = [dft4([x[8 * p1 + p0] for p1 in range(4)], -1) for p0 in range(8)]
    out = []
    for a0 in range(4):
        out += dft8([mul_const(cols[p0][a0], p0 * a0, 32, -1) for p0 in range(8)], -1)
    return out


def dft32_inverse(x):
    rows = [dft8(x[8 * a0 : 8 * a0 + 8], 1) for a0 in range(4)]
    out = [None] * 32
    for p0 in range(8):
        y = dft4([mul_const(rows[a0][p0], p0 * a0, 32, 1) for a0 in range(4)], 1)
        for p1 in range(4):
            out[8 * p1 + p0] = y[p1]
    return out


def dot(x, y, dims):
    return lax.dot_general(x, y, (dims, ((), ())), preferred_element_type=F32)


NN = ((1,), (0,))
NT = ((1,), (1,))


def kernel(
    model, dirty, pb, psf, offs_h, w1h, w2h, w3h, w4h, p1h, p2h, tw1h, tw2h, tw3h,
    res_out, looked,
    model_v, dirty_v, pb_v, psf_v, w1, w2, w3, w4, p1, p2, tw1, tw2, tw3, offs,
    z1, send1, recv1, send2, recv2, psfp, y_v, u_v, z2,
    pbf, sendw, recvw, send3, recv3, send4, buf, rden, joint, res_v,
    lsem, osem, s1, r1, s2, r2, sb, rb_,
):
    bme = lax.axis_index("beam")
    rme = lax.axis_index("row")
    yme, zme = lax.div(rme, 8), lax.rem(rme, 8)
    pair, side = lax.div(bme, 2), lax.rem(bme, 2)

    def row_peer(i):
        dy, dz = (2, 1, 3, 0)[i // 8], (4, 3, 5, 2, 6, 1, 7, 0)[i % 8]
        return lax.rem(yme + dy, 4) * 8 + lax.rem(zme + dz, 8)

    def beam_peer(i):
        return lax.rem(bme + 1 + i, NB)

    def first_row(b):
        return pl.multiple_of(32 * lax.rem(b, 2) + 8 * lax.div(b, 2), 8)

    loads = [
        (model, model_v), (w1h, w1), (tw1h, tw1), (pb, pb_v), (psf, psf_v), (p1h, p1), (p2h, p2),
        (w2h, w2), (w3h, w3), (tw2h, tw2), (w4h, w4), (dirty, dirty_v), (tw3h, tw3), (offs_h, offs),
    ]
    copies = [pltpu.make_async_copy(h, v, lsem.at[i]) for i, (h, v) in enumerate(loads)]
    for c in copies[:3]:
        c.start()

    barrier = pltpu.get_barrier_semaphore()

    for i in range(NR - 1):
        pl.semaphore_signal(barrier, inc=1, device_id=(bme, row_peer(i)), device_id_type=MESH)
    for i in range(NB - 1):
        pl.semaphore_signal(barrier, inc=1, device_id=(beam_peer(i), rme), device_id_type=MESH)
    for c in copies[3:]:
        c.start()

    def send_rows(src, dst, ssem, rsem):
        for i in range(NR - 1):
            peer = row_peer(i)
            pltpu.make_async_remote_copy(
                src_ref=src.at[peer],
                dst_ref=dst.at[rme],
                send_sem=ssem,
                recv_sem=rsem,
                device_id=(bme, peer),
                device_id_type=MESH,
            ).start()
        dst[rme] = src[rme]

    def wait_bytes(part, sem):
        pltpu.make_async_copy(part, part, sem).wait()

    def send_beam(peer, src, dst, ssem, rsem):
        pltpu.make_async_remote_copy(
            src_ref=src,
            dst_ref=dst,
            send_sem=ssem,
            recv_sem=rsem,
            device_id=(peer, rme),
            device_id_type=MESH,
        ).start()

    copies[0].wait()
    copies[1].wait()
    copies[2].wait()
    for half in range(2):
        for rb in range(4):
            for qt in range(2):
                rows = pl.ds(16 * rb, 16)
                x = [model_v[rows, pl.ds(256 * p + 128 * qt, 128)].astype(F32) for p in range(8)]
                if half == 0:
                    s04, s26, s15, s37 = x[0] + x[4], x[2] + x[6], x[1] + x[5], x[3] + x[7]
                    e0, o0 = s04 + s26, s15 + s37
                    y2 = (s04 - s26, s37 - s15)
                    y = {0: (e0 + o0, None), 2: y2, 4: (e0 - o0, None), 6: (y2[0], -y2[1])}
                else:
                    a, b, c, d = x[1] - x[5], x[3] - x[7], x[0] - x[4], x[2] - x[6]
                    u, v = (a - b) * F32(RT), (a + b) * F32(RT)
                    y1, y3 = (c + u, -d - v), (c - u, d - v)
                    y = {1: y1, 3: y3, 5: (y3[0], -y3[1]), 7: (y1[0], -y1[1])}
                for k, (re, im) in y.items():
                    tc = tw1[0, pl.ds(k, 1), pl.ds(128 * qt, 128)]
                    ts = tw1[1, pl.ds(k, 1), pl.ds(128 * qt, 128)]
                    if im is None:
                        zr, zi = re * tc, re * ts
                    else:
                        zr, zi = re * tc - im * ts, re * ts + im * tc
                    to = pl.ds(128 * (FIRST.index(k % 4) % 2) + 64 * (k // 4) + 16 * rb, 16)
                    z1[half, to, pl.ds(128 * qt, 128)] = zr.astype(BF16)
                    z1[half, to, pl.ds(256 + 128 * qt, 128)] = zi.astype(BF16)
        out = dot(w1[...], z1[half], NT).astype(BF16)
        for i in range(2):
            send1[half, :, i] = out[:, 128 * i : 128 * i + 128].reshape(NR, 16, 128)
        if half == 0:
            pl.semaphore_wait(barrier, NR - 1 + NB - 1)
        send_rows(send1.at[half], recv1.at[half], s1.at[half], r1.at[half])

    copies[3].wait()
    for g in range(4):
        both = pb_v[pl.ds(16 * g, 16), :].astype(F32)
        pbf[pl.ds(16 * g, 16), :] = both
        for j in range(2):
            part = both[8 * j : 8 * j + 8]
            to = 2 * ((2 * g + j) % 4) + (2 * g + j) // 4
            sendw[to] = jnp.concatenate([part[:, :1024], part[:, 1024:]], axis=0).astype(BF16)

    for i in range(NB - 1):
        peer = beam_peer(i)
        send_beam(peer, sendw.at[peer], recvw.at[bme], sb.at[0], rb_.at[0])
    recvw[bme] = sendw[bme]

    copies[4].wait()
    copies[5].wait()
    copies[6].wait()
    for m in range(8):
        part = psf_v[:, pl.ds(256 * m, 256)].astype(BF16)
        y_v[:, pl.ds(8 * m, 8), :] = dot(p1[...], part, NT).reshape(32, 8, 128)
    low = lax.broadcasted_iota(jnp.int32, (32, 128), 1) < 64
    for a in range(0, 32, 2):
        two = y_v[pl.ds(a, 2)].reshape(128, 128).astype(BF16)
        got = dot(p2[...], two, NT)
        for c in range(2):
            one, two = got[64 * c : 64 * c + 32], got[64 * c + 32 : 64 * c + 64]
            first = jnp.where(low, one, pltpu.roll(two, 64, 1))
            second = jnp.where(low, pltpu.roll(one, 64, 1), two)
            for t in range(4):
                psfp[t, c, pl.ds(8 * a, 8), :] = first[8 * t : 8 * t + 8]
                psfp[t, c, pl.ds(8 * a + 8, 8), :] = second[8 * t : 8 * t + 8]

    for b in range(NB):
        buf[b, pl.ds(0, 16)] = jnp.zeros((16, 8, 128), F32)
        buf[b, pl.ds(32, 16)] = jnp.zeros((16, 8, 128), F32)

    copies[7].wait()
    copies[8].wait()
    copies[9].wait()
    copies[12].wait()
    copies[13].wait()

    def forward_columns(half, i):
        t = 2 * half + i
        x = []
        for p in range(NR):
            both = recv1[half, p, i].astype(F32)
            x.append((both[:8], both[8:]))
        x = dft32_forward(x)
        for a in range(0, NR, 2):
            turned = [mul(x[a + j], tw2[0, pl.ds(a + j, 1), :], tw2[1, pl.ds(a + j, 1), :]) for j in range(2)]
            for c in range(2):
                z2[t, pl.ds(8 * a, 16), pl.ds(128 * c, 128)] = jnp.concatenate(
                    [turned[0][c], turned[1][c]], axis=0
                ).astype(BF16)
        f = dot(z2[t], w2[...], NN)
        fr, fi = f[:, :128], f[:, 128:]
        pr, pi = psfp[t, 0], psfp[t, 1]
        return [(fr * pr - fi * pi).astype(BF16), (fr * pi + fi * pr).astype(BF16)]

    def inverse_columns(h, half, hi):
        g = dot(h, w3[:, pl.ds(256 * hi, 256)], NN)
        x = []
        for a in range(NR):
            gr, gi = g[8 * a : 8 * a + 8, :128], g[8 * a : 8 * a + 8, 128:]
            x.append(mul((gr, gi), tw3[hi, 0, pl.ds(a, 1), :], tw3[hi, 1, pl.ds(a, 1), :]))
        x = dft32_inverse(x)
        for p in range(NR):
            send2[hi, half, p] = jnp.concatenate([x[p][0], x[p][1]], axis=0).astype(BF16)

    def send_back(half, hi):
        send_rows(send2.at[hi, half], recv2.at[hi, half], s2.at[hi, half], r2.at[hi, half])

    for half in range(2):
        wait_bytes(recv1.at[half, pl.ds(0, NR - 1)], r1.at[half])
        h = jnp.concatenate(forward_columns(half, 0) + forward_columns(half, 1), axis=1)
        for hi in range(2):
            inverse_columns(h, half, hi)
            if half == 1 and hi == 1:
                wait_bytes(recv2.at[0, 1, pl.ds(0, NR - 1)], s2.at[0, 1])
            send_back(half, hi)

    def tile_sum(t):
        total = None
        for b in range(NB):
            one = buf[b, t - offs[b] + 16]
            total = one if total is None else total + one
        return total

    wait_bytes(recvw.at[pl.ds(0, NB - 1)], rb_.at[0])
    for b in range(NB):
        for c in range(8):
            both = recvw[b, :, pl.ds(128 * c, 128)].astype(F32)
            both = both * both
            buf[b, 16 + c] = both[:8]
            buf[b, 24 + c] = both[8:]

    def weigh(t, _):
        rden[t] = 1.0 / jnp.maximum(tile_sum(t), FLOOR)
        return 0

    lax.fori_loop(0, 32, weigh, 0)

    def last(hi, i):
        four = lax.rem(pair + 1 + i, 4)
        owner = 2 * four + hi
        row0 = first_row(owner)
        rows = pl.ds(row0, 8)
        for qt in range(2):
            v = []
            for k in range(8):
                t = FIRST.index(k % 4)
                at = pl.ds(pl.multiple_of(64 * (t % 2) + 32 * (k // 4) + 8 * four, 8), 8)
                ur = u_v[hi, t // 2, at, pl.ds(128 * qt, 128)]
                ui = u_v[hi, t // 2, at, pl.ds(256 + 128 * qt, 128)]
                tc = tw1[0, pl.ds(k, 1), pl.ds(128 * qt, 128)]
                ts = -tw1[1, pl.ds(k, 1), pl.ds(128 * qt, 128)]
                re = ur * tc - ui * ts
                v.append((re, None if k % 4 == 0 else ur * ts + ui * tc))
            s = [None] + [(v[k][0] + v[8 - k][0], v[k][1] - v[8 - k][1]) for k in (1, 2, 3)]
            pp, mm = v[0][0] + v[4][0], v[0][0] - v[4][0]
            e1, e2 = pp + s[2][0], pp - s[2][0]
            o1, o2 = mm - s[2][1], mm + s[2][1]
            f, g = s[1][0] + s[3][0], s[1][1] - s[3][1]
            u = F32(RT) * ((s[1][0] - s[1][1]) - (s[3][0] + s[3][1]))
            w = F32(RT) * ((s[1][0] + s[1][1]) - (s[3][0] - s[3][1]))
            conv = [e1 + f, o1 + u, e2 - g, o2 - w, e1 - f, o1 - u, e2 + g, o2 + w]
            weighted = []
            for p in range(8):
                cols = pl.ds(256 * p + 128 * qt, 128)
                one = dirty_v[rows, cols] - conv[p]
                res_v[rows, cols] = one
                weighted.append(pbf[rows, cols] * one)
            for p in range(4):
                send3[owner, :, pl.ds(256 * p + 128 * qt, 128)] = jnp.concatenate(
                    [weighted[p], weighted[p + 4]], axis=0
                ).astype(BF16)

        @pl.when(owner != bme)
        def _():
            send_beam(owner, send3.at[owner], recv3.at[bme], sb.at[1], rb_.at[1])

    kept = pltpu.make_async_copy(send4.at[bme], looked.at[bme], osem.at[2])

    def joint_rows():
        recv3[bme] = send3[bme]
        wait_bytes(recv3.at[pl.ds(0, NB - 1)], rb_.at[1])
        for b in range(NB):
            for c in range(8):
                both = recv3[b, :, pl.ds(128 * c, 128)].astype(F32)
                buf[b, 16 + c] = both[:8]
                buf[b, 24 + c] = both[8:]

        def join(t, _):
            joint[t] = tile_sum(t) * rden[t]
            return 0

        lax.fori_loop(0, 32, join, 0)

        def reply(i, _):
            b = lax.rem(bme + 1 + i, NB)
            off = offs[b]
            for c in range(8):
                send4[b, :, pl.ds(128 * c, 128)] = jnp.concatenate(
                    [joint[off + c], joint[off + 8 + c]], axis=0
                ).astype(BF16)

            @pl.when(i < NB - 1)
            def _():
                send_beam(b, send4.at[b], looked.at[bme], sb.at[2], rb_.at[2 + side])

            return 0

        lax.fori_loop(0, NB, reply, 0)
        kept.start()

    copies[10].wait()
    copies[11].wait()
    res_copies = []
    for hi in range(2):
        for half in range(2):
            wait_bytes(recv2.at[hi, half, pl.ds(0, NR - 1)], r2.at[hi, half])
            u_v[hi, half] = dot(recv2[hi, half].reshape(512, 128).T, w4[...], NN)

        def go_last(i, _, hi=hi):
            last(hi, i)
            return 0

        lax.fori_loop(0, 4, go_last, 0)
        rows = pl.ds(32 * hi, 32)
        res_copies.append(pltpu.make_async_copy(res_v.at[rows], res_out.at[rows], osem.at[hi]))
        res_copies[hi].start()

    joint_rows()

    for hi in range(2):
        for own, count in ((True, 3), (False, 4)):

            @pl.when((side == hi) == own)
            def _(hi=hi, count=count):
                wait_bytes(looked.at[pl.ds(0, count)], rb_.at[2 + hi])

    for half in range(2):
        wait_bytes(recv1.at[half, pl.ds(0, NR - 1)], s1.at[half])
    for hi, half in ((0, 0), (1, 0), (1, 1)):
        wait_bytes(recv2.at[hi, half, pl.ds(0, NR - 1)], s2.at[hi, half])
    for j in range(3):
        wait_bytes(recvw.at[pl.ds(0, NB - 1)], sb.at[j])
    for c in res_copies:
        c.wait()
    kept.wait()


def finish(res, looked, pb, res_out, ret_out, looked_v, pb_v, ret_v, res_v, isem, osem):
    ins = [
        pltpu.make_async_copy(looked, looked_v, isem.at[0]),
        pltpu.make_async_copy(pb, pb_v, isem.at[1]),
        pltpu.make_async_copy(res, res_v, isem.at[2]),
    ]
    for c in ins:
        c.start()
    ins[0].wait()
    ins[1].wait()
    outs = []
    for hi in range(2):
        for pair in range(2):
            both = pb_v[pl.ds(32 * hi + 16 * pair, 16), :].astype(F32)
            for j in range(2):
                four = 2 * pair + j
                seen = looked_v[2 * four + hi].astype(F32)
                for h in range(2):
                    cols = pl.ds(1024 * h, 1024)
                    ret_v[pl.ds(32 * hi + 8 * four, 8), cols] = (
                        both[8 * j : 8 * j + 8, 1024 * h : 1024 * h + 1024] * seen[8 * h : 8 * h + 8]
                    )
        rows = pl.ds(32 * hi, 32)
        outs.append(pltpu.make_async_copy(ret_v.at[rows], ret_out.at[rows], osem.at[hi]))
        outs[hi].start()
    ins[2].wait()
    outs.append(pltpu.make_async_copy(res_v, res_out, osem.at[2]))
    outs[2].start()
    for c in outs:
        c.wait()


def body(dirty, model, psf_spectrum, primary_beam, offsets):
    consts = [jnp.asarray(v) for v in tables()]
    psf = jnp.swapaxes(psf_spectrum[0], 1, 2).reshape(128, N)
    hbm = pl.BlockSpec(memory_space=pl.ANY)
    image = lambda dt: pltpu.VMEM((ROWS, N), dt)
    rows_in = lambda: pltpu.VMEM((2, NR, 2, 16, 128), BF16)
    rows_out = lambda: pltpu.VMEM((2, 2, NR, 16, 128), BF16)
    beam = lambda: pltpu.VMEM((NB, 16, 1024), BF16)
    scratch = [
        image(BF16), image(F32), image(BF16), pltpu.VMEM((128, N), F32),
        *[pltpu.VMEM(v.shape, v.dtype) for v in consts], pltpu.SMEM((NB,), jnp.int32),
        pltpu.VMEM((2, 256, 512), BF16), rows_in(), rows_in(), rows_out(), rows_out(),
        pltpu.VMEM((4, 2, 256, 128), F32), pltpu.VMEM((32, 64, 128), F32), pltpu.VMEM((2, 2, 128, 512), F32),
        pltpu.VMEM((4, 256, 256), BF16),
        image(F32), beam(), beam(), beam(), beam(), beam(),
        pltpu.VMEM((NB, 48, 8, 128), F32), pltpu.VMEM((32, 8, 128), F32), pltpu.VMEM((32, 8, 128), F32),
        image(F32),
        pltpu.SemaphoreType.DMA((14,)), pltpu.SemaphoreType.DMA((4,)),
        pltpu.SemaphoreType.DMA((2,)), pltpu.SemaphoreType.DMA((2,)),
        pltpu.SemaphoreType.DMA((2, 2)), pltpu.SemaphoreType.DMA((2, 2)),
        pltpu.SemaphoreType.DMA((3,)), pltpu.SemaphoreType.DMA((4,)),
    ]
    residual, looked = pl.pallas_call(
        kernel,
        out_shape=[jax.ShapeDtypeStruct((ROWS, N), F32), jax.ShapeDtypeStruct((NB, 16, 1024), BF16)],
        in_specs=[hbm] * 14,
        out_specs=[hbm] * 2,
        scratch_shapes=scratch,
        compiler_params=pltpu.CompilerParams(
            collective_id=0, has_side_effects=True, vmem_limit_bytes=60 * 1024 * 1024
        ),
    )(model[0], dirty[0], primary_beam[0], psf, offsets, *consts)
    residual, returned = pl.pallas_call(
        finish,
        out_shape=[jax.ShapeDtypeStruct((ROWS, N), F32)] * 2,
        in_specs=[hbm] * 3,
        out_specs=[hbm] * 2,
        scratch_shapes=[
            beam(), image(BF16), image(F32), image(F32),
            pltpu.SemaphoreType.DMA((3,)), pltpu.SemaphoreType.DMA((3,)),
        ],
        compiler_params=pltpu.CompilerParams(vmem_limit_bytes=60 * 1024 * 1024),
    )(residual, looked, primary_beam[0])
    return (residual[None], returned[None])


def solution(mesh):
    in_specs = (
        P("beam", "row", None),
        P("beam", "row", None),
        P("beam", None, None, "row"),
        P("beam", "row", None),
        P(),
    )
    out_specs = (P("beam", "row", None), P("beam", "row", None))
    return jax.shard_map(body, mesh=mesh, in_specs=in_specs, out_specs=out_specs, check_vma=False)
```

```python
import math

import jax
import jax.numpy as jnp
import numpy as np
from jax import lax
from jax.experimental import pallas as pl
from jax.experimental.pallas import tpu as pltpu
from jax.sharding import PartitionSpec as P

MESH = pl.DeviceIdType.MESH
F32 = jnp.float32
BF16 = jnp.bfloat16

N = 2048
ROWS = 64
NR = 32
NB = 8
FIRST = (0, 2, 1, 3)
FLOOR = 0.05
RT = math.sqrt(0.5)


def place(a):
    return 8 * (a % 4) + a // 4


def tables():
    q = np.arange(256)
    k1 = np.arange(8)
    th = 2 * np.pi * (q[None, :] * k1[:, None] % 2048) / 2048
    tw1 = np.stack([np.cos(th), -np.sin(th)]) / math.sqrt(8.0)
    th = 2 * np.pi * (q[:, None] * q[None, :] % 256) / 256
    cos, sin = np.cos(th) / 16, np.sin(th) / 16
    w1 = np.empty((32, 2, 8, 2, 256))
    c3, s3 = cos.reshape(32, 8, 256), sin.reshape(32, 8, 256)
    w1[:, 0, :, 0], w1[:, 0, :, 1] = c3, s3
    w1[:, 1, :, 0], w1[:, 1, :, 1] = -s3, c3
    w4 = np.empty((32, 2, 8, 2, 256))
    w4[:, 0, :, 0], w4[:, 0, :, 1] = c3, s3
    w4[:, 1, :, 0], w4[:, 1, :, 1] = -s3, c3
    r = np.arange(64)
    th = 2 * np.pi * (r[:, None] * r[None, :] % 64) / 64
    cos, sin = np.cos(th) / 8, np.sin(th) / 8
    w2 = np.zeros((2, 2, 64, 2, 2, 64))
    w3 = np.zeros((2, 2, 2, 64, 2, 2, 2, 2, 32))
    for x in range(2):
        w2[0, x, :, 0, x], w2[0, x, :, 1, x] = cos, -sin
        w2[1, x, :, 0, x], w2[1, x, :, 1, x] = sin, cos
        for t in range(2):
            for hi in range(2):
                part = slice(32 * hi, 32 * hi + 32)
                w3[t, 0, x, :, hi, 0, t, x], w3[t, 0, x, :, hi, 1, t, x] = cos[:, part], sin[:, part]
                w3[t, 1, x, :, hi, 0, t, x], w3[t, 1, x, :, hi, 1, t, x] = -sin[:, part], cos[:, part]
    a = np.arange(32)
    th = 2 * np.pi * (r[None, :] * a[:, None] % 2048) / 2048
    tw2 = np.empty((2, 32, 128))
    where = place(a)
    tw2[0, where] = np.tile(np.cos(th), (1, 2)) / math.sqrt(32.0)
    tw2[1, where] = np.tile(-np.sin(th), (1, 2)) / math.sqrt(32.0)
    tw3 = np.empty((2, 2, 32, 128))
    for hi in range(2):
        part = th[:, 32 * hi : 32 * hi + 32]
        tw3[hi, 0, where] = np.tile(np.cos(part), (1, 4)) / math.sqrt(32.0)
        tw3[hi, 1, where] = np.tile(np.sin(part), (1, 4)) / math.sqrt(32.0)
    p1 = np.zeros((256, 256))
    for m in range(8):
        p1[where * 8 + m, 32 * m + a] = 1
    p2 = np.zeros((2, 2, 4, 8, 2, 64))
    for c in range(2):
        for x in range(2):
            for t in range(4):
                for k in range(8):
                    p2[c, x, t, k, c, FIRST[t] + 4 * x + 8 * k] = 1
    bf = lambda v, *s: np.asarray(v.reshape(s), jnp.bfloat16)
    return (
        bf(w1, 512, 512),
        bf(w2, 256, 256),
        bf(w3, 512, 512),
        bf(w4, 512, 512),
        bf(p1, 256, 256),
        bf(p2, 128, 128),
        np.asarray(tw1, np.float32),
        np.asarray(tw2, np.float32),
        np.asarray(tw3, np.float32),
    )


def add(x, y):
    return (x[0] + y[0], x[1] + y[1])


def sub(x, y):
    return (x[0] - y[0], x[1] - y[1])


def turn(x, s):
    return (-x[1], x[0]) if s > 0 else (x[1], -x[0])


def mul(x, c, d):
    return (x[0] * c - x[1] * d, x[0] * d + x[1] * c)


def mul_const(x, num, den, s):
    num %= den
    if num == 0:
        return x
    if 4 * num == den:
        return turn(x, s)
    if 2 * num == den:
        return (-x[0], -x[1])
    if 8 * num == den:
        r = F32(RT)
        return ((x[0] - s * x[1]) * r, (x[1] + s * x[0]) * r)
    if 8 * num == 3 * den:
        r = F32(RT)
        return ((-x[0] - s * x[1]) * r, (s * x[0] - x[1]) * r)
    th = 2 * math.pi * num / den
    return mul(x, F32(math.cos(th)), F32(s * math.sin(th)))


def dft4(x, s):
    t0, t1, t2, t3 = add(x[0], x[2]), sub(x[0], x[2]), add(x[1], x[3]), turn(sub(x[1], x[3]), s)
    return [add(t0, t2), add(t1, t3), sub(t0, t2), sub(t1, t3)]


def dft8(x, s):
    e, o = dft4(x[0::2], s), dft4(x[1::2], s)
    o = [mul_const(o[k], k, 8, s) for k in range(4)]
    return [add(e[k], o[k]) for k in range(4)] + [sub(e[k], o[k]) for k in range(4)]


def dft32_forward(x):
    cols = [dft4([x[8 * p1 + p0] for p1 in range(4)], -1) for p0 in range(8)]
    out = []
    for a0 in range(4):
        out += dft8([mul_const(cols[p0][a0], p0 * a0, 32, -1) for p0 in range(8)], -1)
    return out


def dft32_inverse(x):
    rows = [dft8(x[8 * a0 : 8 * a0 + 8], 1) for a0 in range(4)]
    out = [None] * 32
    for p0 in range(8):
        y = dft4([mul_const(rows[a0][p0], p0 * a0, 32, 1) for a0 in range(4)], 1)
        for p1 in range(4):
            out[8 * p1 + p0] = y[p1]
    return out


def dot(x, y, dims):
    return lax.dot_general(x, y, (dims, ((), ())), preferred_element_type=F32)


NN = ((1,), (0,))
NT = ((1,), (1,))


def kernel(
    model, dirty, pb, psf, offs_h, w1h, w2h, w3h, w4h, p1h, p2h, tw1h, tw2h, tw3h,
    res_out, looked,
    model_v, dirty_v, pb_v, psf_v, w1, w2, w3, w4, p1, p2, tw1, tw2, tw3, offs,
    z1, send1, recv1, send2, recv2, psfp, y_v, u_v, z2,
    pbf, sendw, recvw, send3, recv3, send4, buf, rden, joint, res_v,
    lsem, osem, s1, r1, s2, r2, sb, rb_,
):
    bme = lax.axis_index("beam")
    rme = lax.axis_index("row")
    yme, zme = lax.div(rme, 8), lax.rem(rme, 8)
    pair, side = lax.div(bme, 2), lax.rem(bme, 2)

    def row_peer(i):
        dy, dz = (2, 1, 3, 0)[i // 8], (4, 3, 5, 2, 6, 1, 7, 0)[i % 8]
        return lax.rem(yme + dy, 4) * 8 + lax.rem(zme + dz, 8)

    def beam_peer(i):
        chip = lax.rem(pair + (2, 2, 1, 1, 3, 3, 0, 0)[i], 4)
        return 2 * chip + lax.rem(side + (1 + i) % 2, 2)

    def first_row(b):
        return pl.multiple_of(32 * lax.rem(b, 2) + 8 * lax.div(b, 2), 8)

    loads = [
        (model, model_v), (w1h, w1), (tw1h, tw1), (pb, pb_v), (psf, psf_v), (p1h, p1), (p2h, p2),
        (w2h, w2), (w3h, w3), (tw2h, tw2), (w4h, w4), (dirty, dirty_v), (tw3h, tw3), (offs_h, offs),
    ]
    copies = [pltpu.make_async_copy(h, v, lsem.at[i]) for i, (h, v) in enumerate(loads)]
    for c in copies[:3]:
        c.start()

    barrier = pltpu.get_barrier_semaphore()

    for i in range(NR - 1):
        pl.semaphore_signal(barrier, inc=1, device_id=(bme, row_peer(i)), device_id_type=MESH)
    for i in range(NB - 1):
        pl.semaphore_signal(barrier, inc=1, device_id=(beam_peer(i), rme), device_id_type=MESH)
    for c in copies[3:]:
        c.start()

    def send_rows(src, dst, ssem, rsem):
        for i in range(NR - 1):
            peer = row_peer(i)
            pltpu.make_async_remote_copy(
                src_ref=src.at[peer],
                dst_ref=dst.at[rme],
                send_sem=ssem,
                recv_sem=rsem,
                device_id=(bme, peer),
                device_id_type=MESH,
            ).start()
        dst[rme] = src[rme]

    def wait_bytes(part, sem):
        pltpu.make_async_copy(part, part, sem).wait()

    def send_beam(peer, src, dst, ssem, rsem):
        pltpu.make_async_remote_copy(
            src_ref=src,
            dst_ref=dst,
            send_sem=ssem,
            recv_sem=rsem,
            device_id=(peer, rme),
            device_id_type=MESH,
        ).start()

    copies[0].wait()
    copies[1].wait()
    copies[2].wait()
    for half in range(2):
        for rb in range(4):
            for qt in range(2):
                rows = pl.ds(16 * rb, 16)
                x = [model_v[rows, pl.ds(256 * p + 128 * qt, 128)].astype(F32) for p in range(8)]
                if half == 0:
                    s04, s26, s15, s37 = x[0] + x[4], x[2] + x[6], x[1] + x[5], x[3] + x[7]
                    e0, o0 = s04 + s26, s15 + s37
                    y2 = (s04 - s26, s37 - s15)
                    y = {0: (e0 + o0, None), 2: y2, 4: (e0 - o0, None), 6: (y2[0], -y2[1])}
                else:
                    a, b, c, d = x[1] - x[5], x[3] - x[7], x[0] - x[4], x[2] - x[6]
                    u, v = (a - b) * F32(RT), (a + b) * F32(RT)
                    y1, y3 = (c + u, -d - v), (c - u, d - v)
                    y = {1: y1, 3: y3, 5: (y3[0], -y3[1]), 7: (y1[0], -y1[1])}
                for k, (re, im) in y.items():
                    tc = tw1[0, pl.ds(k, 1), pl.ds(128 * qt, 128)]
                    ts = tw1[1, pl.ds(k, 1), pl.ds(128 * qt, 128)]
                    if im is None:
                        zr, zi = re * tc, re * ts
                    else:
                        zr, zi = re * tc - im * ts, re * ts + im * tc
                    to = pl.ds(128 * (FIRST.index(k % 4) % 2) + 64 * (k // 4) + 16 * rb, 16)
                    z1[half, to, pl.ds(128 * qt, 128)] = zr.astype(BF16)
                    z1[half, to, pl.ds(256 + 128 * qt, 128)] = zi.astype(BF16)
        out = dot(w1[...], z1[half], NT).astype(BF16)
        for i in range(2):
            send1[half, :, i] = out[:, 128 * i : 128 * i + 128].reshape(NR, 16, 128)
        if half == 0:
            pl.semaphore_wait(barrier, NR - 1 + NB - 1)
        send_rows(send1.at[half], recv1.at[half], s1.at[half], r1.at[half])

    copies[3].wait()
    for g in range(4):
        both = pb_v[pl.ds(16 * g, 16), :].astype(F32)
        pbf[pl.ds(16 * g, 16), :] = both
        for j in range(2):
            part = both[8 * j : 8 * j + 8]
            to = 2 * ((2 * g + j) % 4) + (2 * g + j) // 4
            sendw[to] = jnp.concatenate([part[:, :1024], part[:, 1024:]], axis=0).astype(BF16)

    for i in range(NB - 1):
        peer = beam_peer(i)
        send_beam(peer, sendw.at[peer], recvw.at[bme], sb.at[0], rb_.at[0])
    recvw[bme] = sendw[bme]

    copies[4].wait()
    copies[5].wait()
    copies[6].wait()
    for m in range(8):
        part = psf_v[:, pl.ds(256 * m, 256)].astype(BF16)
        y_v[:, pl.ds(8 * m, 8), :] = dot(p1[...], part, NT).reshape(32, 8, 128)
    low = lax.broadcasted_iota(jnp.int32, (32, 128), 1) < 64
    for a in range(0, 32, 2):
        two = y_v[pl.ds(a, 2)].reshape(128, 128).astype(BF16)
        got = dot(p2[...], two, NT)
        for c in range(2):
            one, two = got[64 * c : 64 * c + 32], got[64 * c + 32 : 64 * c + 64]
            first = jnp.where(low, one, pltpu.roll(two, 64, 1))
            second = jnp.where(low, pltpu.roll(one, 64, 1), two)
            for t in range(4):
                psfp[t, c, pl.ds(8 * a, 8), :] = first[8 * t : 8 * t + 8]
                psfp[t, c, pl.ds(8 * a + 8, 8), :] = second[8 * t : 8 * t + 8]

    for b in range(NB):
        buf[b, pl.ds(0, 16)] = jnp.zeros((16, 8, 128), F32)
        buf[b, pl.ds(32, 16)] = jnp.zeros((16, 8, 128), F32)

    copies[7].wait()
    copies[8].wait()
    copies[9].wait()
    copies[12].wait()
    copies[13].wait()

    def forward_columns(half, i):
        t = 2 * half + i
        x = []
        for p in range(NR):
            both = recv1[half, p, i].astype(F32)
            x.append((both[:8], both[8:]))
        x = dft32_forward(x)
        for a in range(0, NR, 2):
            turned = [mul(x[a + j], tw2[0, pl.ds(a + j, 1), :], tw2[1, pl.ds(a + j, 1), :]) for j in range(2)]
            for c in range(2):
                z2[t, pl.ds(8 * a, 16), pl.ds(128 * c, 128)] = jnp.concatenate(
                    [turned[0][c], turned[1][c]], axis=0
                ).astype(BF16)
        f = dot(z2[t], w2[...], NN)
        fr, fi = f[:, :128], f[:, 128:]
        pr, pi = psfp[t, 0], psfp[t, 1]
        return [(fr * pr - fi * pi).astype(BF16), (fr * pi + fi * pr).astype(BF16)]

    def inverse_columns(h, half, hi):
        g = dot(h, w3[:, pl.ds(256 * hi, 256)], NN)
        x = []
        for a in range(NR):
            gr, gi = g[8 * a : 8 * a + 8, :128], g[8 * a : 8 * a + 8, 128:]
            x.append(mul((gr, gi), tw3[hi, 0, pl.ds(a, 1), :], tw3[hi, 1, pl.ds(a, 1), :]))
        x = dft32_inverse(x)
        for p in range(NR):
            send2[hi, half, p] = jnp.concatenate([x[p][0], x[p][1]], axis=0).astype(BF16)

    def send_back(half, hi):
        send_rows(send2.at[hi, half], recv2.at[hi, half], s2.at[hi, half], r2.at[hi, half])

    for half in range(2):
        wait_bytes(recv1.at[half, pl.ds(0, NR - 1)], r1.at[half])
        h = jnp.concatenate(forward_columns(half, 0) + forward_columns(half, 1), axis=1)
        for hi in range(2):
            inverse_columns(h, half, hi)
            if half == 1 and hi == 1:
                wait_bytes(recv2.at[0, 1, pl.ds(0, NR - 1)], s2.at[0, 1])
            send_back(half, hi)

    starts = [16 - offs[b] for b in range(NB)]

    def tile_sum(t):
        ones = [buf[b, starts[b] + t] for b in range(NB)]
        while len(ones) > 1:
            ones = [ones[k] + ones[k + 1] for k in range(0, len(ones), 2)]
        return ones[0]

    wait_bytes(recvw.at[pl.ds(0, NB - 1)], rb_.at[0])
    for b in range(NB):
        for c in range(8):
            both = recvw[b, :, pl.ds(128 * c, 128)].astype(F32)
            both = both * both
            buf[b, 16 + c] = both[:8]
            buf[b, 24 + c] = both[8:]

    def weigh(t, _):
        rden[t] = 1.0 / jnp.maximum(tile_sum(t), FLOOR)
        return 0

    lax.fori_loop(0, 32, weigh, 0)

    def last(hi, i):
        four = lax.rem(pair + (2, 1, 3, 0)[i], 4)
        owner = 2 * four + hi
        row0 = first_row(owner)
        rows = pl.ds(row0, 8)
        for qt in range(2):
            v = []
            for k in range(8):
                t = FIRST.index(k % 4)
                at = pl.ds(pl.multiple_of(64 * (t % 2) + 32 * (k // 4) + 8 * four, 8), 8)
                ur = u_v[hi, t // 2, at, pl.ds(128 * qt, 128)]
                ui = u_v[hi, t // 2, at, pl.ds(256 + 128 * qt, 128)]
                tc = tw1[0, pl.ds(k, 1), pl.ds(128 * qt, 128)]
                ts = -tw1[1, pl.ds(k, 1), pl.ds(128 * qt, 128)]
                re = ur * tc - ui * ts
                v.append((re, None if k % 4 == 0 else ur * ts + ui * tc))
            s = [None] + [(v[k][0] + v[8 - k][0], v[k][1] - v[8 - k][1]) for k in (1, 2, 3)]
            pp, mm = v[0][0] + v[4][0], v[0][0] - v[4][0]
            e1, e2 = pp + s[2][0], pp - s[2][0]
            o1, o2 = mm - s[2][1], mm + s[2][1]
            f, g = s[1][0] + s[3][0], s[1][1] - s[3][1]
            u = F32(RT) * ((s[1][0] - s[1][1]) - (s[3][0] + s[3][1]))
            w = F32(RT) * ((s[1][0] + s[1][1]) - (s[3][0] - s[3][1]))
            conv = [e1 + f, o1 + u, e2 - g, o2 - w, e1 - f, o1 - u, e2 + g, o2 + w]
            weighted = []
            for p in range(8):
                cols = pl.ds(256 * p + 128 * qt, 128)
                one = dirty_v[rows, cols] - conv[p]
                res_v[rows, cols] = one
                weighted.append(pbf[rows, cols] * one)
            for p in range(4):
                send3[owner, :, pl.ds(256 * p + 128 * qt, 128)] = jnp.concatenate(
                    [weighted[p], weighted[p + 4]], axis=0
                ).astype(BF16)

        @pl.when(owner != bme)
        def _():
            send_beam(owner, send3.at[owner], recv3.at[bme], sb.at[1], rb_.at[1])

    kept = pltpu.make_async_copy(send4.at[bme], looked.at[bme], osem.at[2])

    def joint_rows():
        recv3[bme] = send3[bme]
        wait_bytes(recv3.at[pl.ds(0, NB - 1)], rb_.at[1])
        for b in range(NB):
            for c in range(8):
                both = recv3[b, :, pl.ds(128 * c, 128)].astype(F32)
                buf[b, 16 + c] = both[:8]
                buf[b, 24 + c] = both[8:]

        for t in range(32):
            joint[t] = tile_sum(t) * rden[t]
        for i in range(NB):
            b = beam_peer(i)
            off = offs[b]
            for c in range(8):
                send4[b, :, pl.ds(128 * c, 128)] = jnp.concatenate(
                    [joint[off + c], joint[off + 8 + c]], axis=0
                ).astype(BF16)
            if i < NB - 1:
                send_beam(b, send4.at[b], looked.at[bme], sb.at[2], rb_.at[2 + side])
        kept.start()

    copies[10].wait()
    copies[11].wait()
    res_copies = []
    for hi in range(2):
        for half in range(2):
            wait_bytes(recv2.at[hi, half, pl.ds(0, NR - 1)], r2.at[hi, half])
            u_v[hi, half] = dot(recv2[hi, half].reshape(512, 128).T, w4[...], NN)

        for i in range(4):
            last(hi, i)
        rows = pl.ds(32 * hi, 32)
        res_copies.append(pltpu.make_async_copy(res_v.at[rows], res_out.at[rows], osem.at[hi]))
        res_copies[hi].start()

    joint_rows()

    for hi in range(2):
        for own, count in ((True, 3), (False, 4)):

            @pl.when((side == hi) == own)
            def _(hi=hi, count=count):
                wait_bytes(looked.at[pl.ds(0, count)], rb_.at[2 + hi])

    for half in range(2):
        wait_bytes(recv1.at[half, pl.ds(0, NR - 1)], s1.at[half])
    for hi, half in ((0, 0), (1, 0), (1, 1)):
        wait_bytes(recv2.at[hi, half, pl.ds(0, NR - 1)], s2.at[hi, half])
    for j in range(3):
        wait_bytes(recvw.at[pl.ds(0, NB - 1)], sb.at[j])
    for c in res_copies:
        c.wait()
    kept.wait()


def finish(res, looked, pb, res_out, ret_out, looked_v, pb_v, ret_v, res_v, isem, osem):
    ins = [
        pltpu.make_async_copy(looked, looked_v, isem.at[0]),
        pltpu.make_async_copy(pb, pb_v, isem.at[1]),
        pltpu.make_async_copy(res, res_v, isem.at[2]),
    ]
    for c in ins:
        c.start()
    ins[0].wait()
    ins[1].wait()
    outs = []
    for hi in range(2):
        for pair in range(2):
            both = pb_v[pl.ds(32 * hi + 16 * pair, 16), :].astype(F32)
            for j in range(2):
                four = 2 * pair + j
                seen = looked_v[2 * four + hi].astype(F32)
                for h in range(2):
                    cols = pl.ds(1024 * h, 1024)
                    ret_v[pl.ds(32 * hi + 8 * four, 8), cols] = (
                        both[8 * j : 8 * j + 8, 1024 * h : 1024 * h + 1024] * seen[8 * h : 8 * h + 8]
                    )
        rows = pl.ds(32 * hi, 32)
        outs.append(pltpu.make_async_copy(ret_v.at[rows], ret_out.at[rows], osem.at[hi]))
        outs[hi].start()
    ins[2].wait()
    outs.append(pltpu.make_async_copy(res_v, res_out, osem.at[2]))
    outs[2].start()
    for c in outs:
        c.wait()


def body(dirty, model, psf_spectrum, primary_beam, offsets):
    consts = [jnp.asarray(v) for v in tables()]
    psf = jnp.swapaxes(psf_spectrum[0], 1, 2).reshape(128, N)
    hbm = pl.BlockSpec(memory_space=pl.ANY)
    image = lambda dt: pltpu.VMEM((ROWS, N), dt)
    rows_in = lambda: pltpu.VMEM((2, NR, 2, 16, 128), BF16)
    rows_out = lambda: pltpu.VMEM((2, 2, NR, 16, 128), BF16)
    beam = lambda: pltpu.VMEM((NB, 16, 1024), BF16)
    scratch = [
        image(BF16), image(F32), image(BF16), pltpu.VMEM((128, N), F32),
        *[pltpu.VMEM(v.shape, v.dtype) for v in consts], pltpu.SMEM((NB,), jnp.int32),
        pltpu.VMEM((2, 256, 512), BF16), rows_in(), rows_in(), rows_out(), rows_out(),
        pltpu.VMEM((4, 2, 256, 128), F32), pltpu.VMEM((32, 64, 128), F32), pltpu.VMEM((2, 2, 128, 512), F32),
        pltpu.VMEM((4, 256, 256), BF16),
        image(F32), beam(), beam(), beam(), beam(), beam(),
        pltpu.VMEM((NB, 48, 8, 128), F32), pltpu.VMEM((32, 8, 128), F32), pltpu.VMEM((32, 8, 128), F32),
        image(F32),
        pltpu.SemaphoreType.DMA((14,)), pltpu.SemaphoreType.DMA((4,)),
        pltpu.SemaphoreType.DMA((2,)), pltpu.SemaphoreType.DMA((2,)),
        pltpu.SemaphoreType.DMA((2, 2)), pltpu.SemaphoreType.DMA((2, 2)),
        pltpu.SemaphoreType.DMA((3,)), pltpu.SemaphoreType.DMA((4,)),
    ]
    residual, looked = pl.pallas_call(
        kernel,
        out_shape=[jax.ShapeDtypeStruct((ROWS, N), F32), jax.ShapeDtypeStruct((NB, 16, 1024), BF16)],
        in_specs=[hbm] * 14,
        out_specs=[hbm] * 2,
        scratch_shapes=scratch,
        compiler_params=pltpu.CompilerParams(
            collective_id=0, has_side_effects=True, vmem_limit_bytes=60 * 1024 * 1024
        ),
    )(model[0], dirty[0], primary_beam[0], psf, offsets, *consts)
    residual, returned = pl.pallas_call(
        finish,
        out_shape=[jax.ShapeDtypeStruct((ROWS, N), F32)] * 2,
        in_specs=[hbm] * 3,
        out_specs=[hbm] * 2,
        scratch_shapes=[
            beam(), image(BF16), image(F32), image(F32),
            pltpu.SemaphoreType.DMA((3,)), pltpu.SemaphoreType.DMA((3,)),
        ],
        compiler_params=pltpu.CompilerParams(vmem_limit_bytes=60 * 1024 * 1024),
    )(residual, looked, primary_beam[0])
    return (residual[None], returned[None])


def solution(mesh):
    in_specs = (
        P("beam", "row", None),
        P("beam", "row", None),
        P("beam", None, None, "row"),
        P("beam", "row", None),
        P(),
    )
    out_specs = (P("beam", "row", None), P("beam", "row", None))
    return jax.shard_map(body, mesh=mesh, in_specs=in_specs, out_specs=out_specs, check_vma=False)
```

```python
import math

import jax
import jax.numpy as jnp
import numpy as np
from jax import lax
from jax.experimental import pallas as pl
from jax.experimental.pallas import tpu as pltpu
from jax.sharding import PartitionSpec as P

MESH = pl.DeviceIdType.MESH
F32 = jnp.float32
BF16 = jnp.bfloat16

N = 2048
ROWS = 64
NR = 32
NB = 8
FIRST = (0, 2, 1, 3)
FLOOR = 0.05
RT = math.sqrt(0.5)


def place(a):
    return 8 * (a % 4) + a // 4


def tables():
    q = np.arange(256)
    k1 = np.arange(8)
    th = 2 * np.pi * (q[None, :] * k1[:, None] % 2048) / 2048
    tw1 = np.stack([np.cos(th), -np.sin(th)]) / math.sqrt(8.0)
    th = 2 * np.pi * (q[:, None] * q[None, :] % 256) / 256
    cos, sin = np.cos(th) / 16, np.sin(th) / 16
    w1 = np.empty((32, 2, 8, 2, 256))
    c3, s3 = cos.reshape(32, 8, 256), sin.reshape(32, 8, 256)
    w1[:, 0, :, 0], w1[:, 0, :, 1] = c3, s3
    w1[:, 1, :, 0], w1[:, 1, :, 1] = -s3, c3
    w4 = np.empty((32, 2, 8, 2, 256))
    w4[:, 0, :, 0], w4[:, 0, :, 1] = c3, s3
    w4[:, 1, :, 0], w4[:, 1, :, 1] = -s3, c3
    r = np.arange(64)
    th = 2 * np.pi * (r[:, None] * r[None, :] % 64) / 64
    cos, sin = np.cos(th) / 8, np.sin(th) / 8
    w2 = np.zeros((2, 2, 64, 2, 2, 64))
    w3 = np.zeros((2, 2, 2, 64, 2, 2, 2, 2, 32))
    for x in range(2):
        w2[0, x, :, 0, x], w2[0, x, :, 1, x] = cos, -sin
        w2[1, x, :, 0, x], w2[1, x, :, 1, x] = sin, cos
        for t in range(2):
            for hi in range(2):
                part = slice(32 * hi, 32 * hi + 32)
                w3[t, 0, x, :, hi, 0, t, x], w3[t, 0, x, :, hi, 1, t, x] = cos[:, part], sin[:, part]
                w3[t, 1, x, :, hi, 0, t, x], w3[t, 1, x, :, hi, 1, t, x] = -sin[:, part], cos[:, part]
    a = np.arange(32)
    th = 2 * np.pi * (r[None, :] * a[:, None] % 2048) / 2048
    tw2 = np.empty((2, 32, 128))
    where = place(a)
    tw2[0, where] = np.tile(np.cos(th), (1, 2)) / math.sqrt(32.0)
    tw2[1, where] = np.tile(-np.sin(th), (1, 2)) / math.sqrt(32.0)
    tw3 = np.empty((2, 2, 32, 128))
    for hi in range(2):
        part = th[:, 32 * hi : 32 * hi + 32]
        tw3[hi, 0, where] = np.tile(np.cos(part), (1, 4)) / math.sqrt(32.0)
        tw3[hi, 1, where] = np.tile(np.sin(part), (1, 4)) / math.sqrt(32.0)
    p1 = np.zeros((256, 256))
    for m in range(8):
        p1[where * 8 + m, 32 * m + a] = 1
    p2 = np.zeros((2, 2, 4, 8, 2, 64))
    for c in range(2):
        for x in range(2):
            for t in range(4):
                for k in range(8):
                    p2[c, x, t, k, c, FIRST[t] + 4 * x + 8 * k] = 1
    bf = lambda v, *s: np.asarray(v.reshape(s), jnp.bfloat16)
    return (
        bf(w1, 512, 512),
        bf(w2, 256, 256),
        bf(w3, 512, 512),
        bf(w4, 512, 512),
        bf(p1, 256, 256),
        bf(p2, 128, 128),
        np.asarray(tw1, np.float32),
        np.asarray(tw2, np.float32),
        np.asarray(tw3, np.float32),
    )


def add(x, y):
    return (x[0] + y[0], x[1] + y[1])


def sub(x, y):
    return (x[0] - y[0], x[1] - y[1])


def turn(x, s):
    return (-x[1], x[0]) if s > 0 else (x[1], -x[0])


def mul(x, c, d):
    return (x[0] * c - x[1] * d, x[0] * d + x[1] * c)


def mul_const(x, num, den, s):
    num %= den
    if num == 0:
        return x
    if 4 * num == den:
        return turn(x, s)
    if 2 * num == den:
        return (-x[0], -x[1])
    if 8 * num == den:
        r = F32(RT)
        return ((x[0] - s * x[1]) * r, (x[1] + s * x[0]) * r)
    if 8 * num == 3 * den:
        r = F32(RT)
        return ((-x[0] - s * x[1]) * r, (s * x[0] - x[1]) * r)
    th = 2 * math.pi * num / den
    return mul(x, F32(math.cos(th)), F32(s * math.sin(th)))


def dft4(x, s):
    t0, t1, t2, t3 = add(x[0], x[2]), sub(x[0], x[2]), add(x[1], x[3]), turn(sub(x[1], x[3]), s)
    return [add(t0, t2), add(t1, t3), sub(t0, t2), sub(t1, t3)]


def dft8(x, s):
    e, o = dft4(x[0::2], s), dft4(x[1::2], s)
    o = [mul_const(o[k], k, 8, s) for k in range(4)]
    return [add(e[k], o[k]) for k in range(4)] + [sub(e[k], o[k]) for k in range(4)]


def dft32_forward(x):
    cols = [dft4([x[8 * p1 + p0] for p1 in range(4)], -1) for p0 in range(8)]
    out = []
    for a0 in range(4):
        out += dft8([mul_const(cols[p0][a0], p0 * a0, 32, -1) for p0 in range(8)], -1)
    return out


def dft32_inverse(x):
    rows = [dft8(x[8 * a0 : 8 * a0 + 8], 1) for a0 in range(4)]
    out = [None] * 32
    for p0 in range(8):
        y = dft4([mul_const(rows[a0][p0], p0 * a0, 32, 1) for a0 in range(4)], 1)
        for p1 in range(4):
            out[8 * p1 + p0] = y[p1]
    return out


def dot(x, y, dims):
    return lax.dot_general(x, y, (dims, ((), ())), preferred_element_type=F32)


NN = ((1,), (0,))
NT = ((1,), (1,))


def kernel(
    model, dirty, pb, psf, offs_h, w1h, w2h, w3h, w4h, p1h, p2h, tw1h, tw2h, tw3h,
    res_v, looked, pbf,
    model_v, dirty_v, pb_v, psf_v, w1, w2, w3, w4, p1, p2, tw1, tw2, tw3, offs,
    z1, send1, recv1, send2, recv2, psfp, y_v, u_v, z2,
    sendw, recvw, send3, recv3, send4, buf, rden, joint,
    lsem, osem, s1, r1, s2, r2, sb, rb_,
):
    bme = lax.axis_index("beam")
    rme = lax.axis_index("row")
    yme, zme = lax.div(rme, 8), lax.rem(rme, 8)
    pair, side = lax.div(bme, 2), lax.rem(bme, 2)

    def row_peer(i):
        dy, dz = (2, 1, 3, 0)[i // 8], (4, 3, 5, 2, 6, 1, 7, 0)[i % 8]
        return lax.rem(yme + dy, 4) * 8 + lax.rem(zme + dz, 8)

    def beam_peer(i):
        chip = lax.rem(pair + (2, 2, 1, 1, 3, 3, 0, 0)[i], 4)
        return 2 * chip + lax.rem(side + (1 + i) % 2, 2)

    def first_row(b):
        return pl.multiple_of(32 * lax.rem(b, 2) + 8 * lax.div(b, 2), 8)

    loads = [
        (model, model_v), (w1h, w1), (tw1h, tw1), (pb, pb_v), (psf, psf_v), (p1h, p1), (p2h, p2),
        (w2h, w2), (w3h, w3), (tw2h, tw2), (w4h, w4), (dirty, dirty_v), (tw3h, tw3), (offs_h, offs),
    ]
    copies = [pltpu.make_async_copy(h, v, lsem.at[i]) for i, (h, v) in enumerate(loads)]
    for c in copies[:3]:
        c.start()

    barrier = pltpu.get_barrier_semaphore()

    for i in range(NR - 1):
        pl.semaphore_signal(barrier, inc=1, device_id=(bme, row_peer(i)), device_id_type=MESH)
    for i in range(NB - 1):
        pl.semaphore_signal(barrier, inc=1, device_id=(beam_peer(i), rme), device_id_type=MESH)
    for c in copies[3:]:
        c.start()

    def send_rows(src, dst, ssem, rsem):
        for i in range(NR - 1):
            peer = row_peer(i)
            pltpu.make_async_remote_copy(
                src_ref=src.at[peer],
                dst_ref=dst.at[rme],
                send_sem=ssem,
                recv_sem=rsem,
                device_id=(bme, peer),
                device_id_type=MESH,
            ).start()
        dst[rme] = src[rme]

    def wait_bytes(part, sem):
        pltpu.make_async_copy(part, part, sem).wait()

    def send_beam(peer, src, dst, ssem, rsem):
        pltpu.make_async_remote_copy(
            src_ref=src,
            dst_ref=dst,
            send_sem=ssem,
            recv_sem=rsem,
            device_id=(peer, rme),
            device_id_type=MESH,
        ).start()

    copies[0].wait()
    copies[1].wait()
    copies[2].wait()
    for half in range(2):
        for rb in range(4):
            for qt in range(2):
                rows = pl.ds(16 * rb, 16)
                x = [model_v[rows, pl.ds(256 * p + 128 * qt, 128)].astype(F32) for p in range(8)]
                if half == 0:
                    s04, s26, s15, s37 = x[0] + x[4], x[2] + x[6], x[1] + x[5], x[3] + x[7]
                    e0, o0 = s04 + s26, s15 + s37
                    y2 = (s04 - s26, s37 - s15)
                    y = {0: (e0 + o0, None), 2: y2, 4: (e0 - o0, None), 6: (y2[0], -y2[1])}
                else:
                    a, b, c, d = x[1] - x[5], x[3] - x[7], x[0] - x[4], x[2] - x[6]
                    u, v = (a - b) * F32(RT), (a + b) * F32(RT)
                    y1, y3 = (c + u, -d - v), (c - u, d - v)
                    y = {1: y1, 3: y3, 5: (y3[0], -y3[1]), 7: (y1[0], -y1[1])}
                for k, (re, im) in y.items():
                    tc = tw1[0, pl.ds(k, 1), pl.ds(128 * qt, 128)]
                    ts = tw1[1, pl.ds(k, 1), pl.ds(128 * qt, 128)]
                    if im is None:
                        zr, zi = re * tc, re * ts
                    else:
                        zr, zi = re * tc - im * ts, re * ts + im * tc
                    to = pl.ds(128 * (FIRST.index(k % 4) % 2) + 64 * (k // 4) + 16 * rb, 16)
                    z1[half, to, pl.ds(128 * qt, 128)] = zr.astype(BF16)
                    z1[half, to, pl.ds(256 + 128 * qt, 128)] = zi.astype(BF16)
        out = dot(w1[...], z1[half], NT).astype(BF16)
        for i in range(2):
            send1[half, :, i] = out[:, 128 * i : 128 * i + 128].reshape(NR, 16, 128)
        if half == 0:
            pl.semaphore_wait(barrier, NR - 1 + NB - 1)
        send_rows(send1.at[half], recv1.at[half], s1.at[half], r1.at[half])

    copies[3].wait()
    for g in range(4):
        both = pb_v[pl.ds(16 * g, 16), :].astype(F32)
        pbf[pl.ds(16 * g, 16), :] = both
        for j in range(2):
            part = both[8 * j : 8 * j + 8]
            to = 2 * ((2 * g + j) % 4) + (2 * g + j) // 4
            sendw[to] = jnp.concatenate([part[:, :1024], part[:, 1024:]], axis=0).astype(BF16)

    for i in range(NB - 1):
        peer = beam_peer(i)
        send_beam(peer, sendw.at[peer], recvw.at[bme], sb.at[0], rb_.at[0])
    recvw[bme] = sendw[bme]

    copies[4].wait()
    copies[5].wait()
    copies[6].wait()
    for m in range(8):
        part = psf_v[:, pl.ds(256 * m, 256)].astype(BF16)
        y_v[:, pl.ds(8 * m, 8), :] = dot(p1[...], part, NT).reshape(32, 8, 128)
    low = lax.broadcasted_iota(jnp.int32, (32, 128), 1) < 64
    for a in range(0, 32, 2):
        two = y_v[pl.ds(a, 2)].reshape(128, 128).astype(BF16)
        got = dot(p2[...], two, NT)
        for c in range(2):
            one, two = got[64 * c : 64 * c + 32], got[64 * c + 32 : 64 * c + 64]
            first = jnp.where(low, one, pltpu.roll(two, 64, 1))
            second = jnp.where(low, pltpu.roll(one, 64, 1), two)
            for t in range(4):
                psfp[t, c, pl.ds(8 * a, 8), :] = first[8 * t : 8 * t + 8]
                psfp[t, c, pl.ds(8 * a + 8, 8), :] = second[8 * t : 8 * t + 8]

    for b in range(NB):
        buf[b, pl.ds(0, 16)] = jnp.zeros((16, 8, 128), F32)
        buf[b, pl.ds(32, 16)] = jnp.zeros((16, 8, 128), F32)

    copies[7].wait()
    copies[8].wait()
    copies[9].wait()
    copies[12].wait()
    copies[13].wait()

    def forward_columns(half, i):
        t = 2 * half + i
        x = []
        for p in range(NR):
            both = recv1[half, p, i].astype(F32)
            x.append((both[:8], both[8:]))
        x = dft32_forward(x)
        for a in range(0, NR, 2):
            turned = [mul(x[a + j], tw2[0, pl.ds(a + j, 1), :], tw2[1, pl.ds(a + j, 1), :]) for j in range(2)]
            for c in range(2):
                z2[t, pl.ds(8 * a, 16), pl.ds(128 * c, 128)] = jnp.concatenate(
                    [turned[0][c], turned[1][c]], axis=0
                ).astype(BF16)
        f = dot(z2[t], w2[...], NN)
        fr, fi = f[:, :128], f[:, 128:]
        pr, pi = psfp[t, 0], psfp[t, 1]
        return [(fr * pr - fi * pi).astype(BF16), (fr * pi + fi * pr).astype(BF16)]

    def inverse_columns(h, half, hi):
        g = dot(h, w3[:, pl.ds(256 * hi, 256)], NN)
        x = []
        for a in range(NR):
            gr, gi = g[8 * a : 8 * a + 8, :128], g[8 * a : 8 * a + 8, 128:]
            x.append(mul((gr, gi), tw3[hi, 0, pl.ds(a, 1), :], tw3[hi, 1, pl.ds(a, 1), :]))
        x = dft32_inverse(x)
        for p in range(NR):
            send2[hi, half, p] = jnp.concatenate([x[p][0], x[p][1]], axis=0).astype(BF16)

    def send_back(half, hi):
        send_rows(send2.at[hi, half], recv2.at[hi, half], s2.at[hi, half], r2.at[hi, half])

    for half in range(2):
        wait_bytes(recv1.at[half, pl.ds(0, NR - 1)], r1.at[half])
        h = jnp.concatenate(forward_columns(half, 0) + forward_columns(half, 1), axis=1)
        for hi in range(2):
            inverse_columns(h, half, hi)
            if half == 1 and hi == 1:
                wait_bytes(recv2.at[0, 1, pl.ds(0, NR - 1)], s2.at[0, 1])
            send_back(half, hi)

    starts = [16 - offs[b] for b in range(NB)]

    def tile_sum(t):
        ones = [buf[b, starts[b] + t] for b in range(NB)]
        while len(ones) > 1:
            ones = [ones[k] + ones[k + 1] for k in range(0, len(ones), 2)]
        return ones[0]

    wait_bytes(recvw.at[pl.ds(0, NB - 1)], rb_.at[0])
    for b in range(NB):
        for c in range(8):
            both = recvw[b, :, pl.ds(128 * c, 128)].astype(F32)
            both = both * both
            buf[b, 16 + c] = both[:8]
            buf[b, 24 + c] = both[8:]

    def weigh(t, _):
        rden[t] = 1.0 / jnp.maximum(tile_sum(t), FLOOR)
        return 0

    lax.fori_loop(0, 32, weigh, 0)

    def last(hi, i):
        four = lax.rem(pair + (2, 1, 3, 0)[i], 4)
        owner = 2 * four + hi
        row0 = first_row(owner)
        rows = pl.ds(row0, 8)
        for qt in range(2):
            v = []
            for k in range(8):
                t = FIRST.index(k % 4)
                at = pl.ds(pl.multiple_of(64 * (t % 2) + 32 * (k // 4) + 8 * four, 8), 8)
                ur = u_v[hi, t // 2, at, pl.ds(128 * qt, 128)]
                ui = u_v[hi, t // 2, at, pl.ds(256 + 128 * qt, 128)]
                tc = tw1[0, pl.ds(k, 1), pl.ds(128 * qt, 128)]
                ts = -tw1[1, pl.ds(k, 1), pl.ds(128 * qt, 128)]
                re = ur * tc - ui * ts
                v.append((re, None if k % 4 == 0 else ur * ts + ui * tc))
            s = [None] + [(v[k][0] + v[8 - k][0], v[k][1] - v[8 - k][1]) for k in (1, 2, 3)]
            pp, mm = v[0][0] + v[4][0], v[0][0] - v[4][0]
            e1, e2 = pp + s[2][0], pp - s[2][0]
            o1, o2 = mm - s[2][1], mm + s[2][1]
            f, g = s[1][0] + s[3][0], s[1][1] - s[3][1]
            u = F32(RT) * ((s[1][0] - s[1][1]) - (s[3][0] + s[3][1]))
            w = F32(RT) * ((s[1][0] + s[1][1]) - (s[3][0] - s[3][1]))
            conv = [e1 + f, o1 + u, e2 - g, o2 - w, e1 - f, o1 - u, e2 + g, o2 + w]
            weighted = []
            for p in range(8):
                cols = pl.ds(256 * p + 128 * qt, 128)
                one = dirty_v[rows, cols] - conv[p]
                res_v[rows, cols] = one
                weighted.append(pbf[rows, cols] * one)
            for p in range(4):
                send3[owner, :, pl.ds(256 * p + 128 * qt, 128)] = jnp.concatenate(
                    [weighted[p], weighted[p + 4]], axis=0
                ).astype(BF16)

        @pl.when(owner != bme)
        def _():
            send_beam(owner, send3.at[owner], recv3.at[bme], sb.at[1], rb_.at[1])

    kept = pltpu.make_async_copy(send4.at[bme], looked.at[bme], osem)

    def joint_rows():
        recv3[bme] = send3[bme]
        wait_bytes(recv3.at[pl.ds(0, NB - 1)], rb_.at[1])
        for b in range(NB):
            for c in range(8):
                both = recv3[b, :, pl.ds(128 * c, 128)].astype(F32)
                buf[b, 16 + c] = both[:8]
                buf[b, 24 + c] = both[8:]

        for t in range(32):
            joint[t] = tile_sum(t) * rden[t]
        for i in range(NB):
            b = beam_peer(i)
            off = offs[b]
            for c in range(8):
                send4[b, :, pl.ds(128 * c, 128)] = jnp.concatenate(
                    [joint[off + c], joint[off + 8 + c]], axis=0
                ).astype(BF16)
            if i < NB - 1:
                send_beam(b, send4.at[b], looked.at[bme], sb.at[2], rb_.at[2 + side])
        kept.start()

    copies[10].wait()
    copies[11].wait()
    for hi in range(2):
        for half in range(2):
            wait_bytes(recv2.at[hi, half, pl.ds(0, NR - 1)], r2.at[hi, half])
            u_v[hi, half] = dot(recv2[hi, half].reshape(512, 128).T, w4[...], NN)

        for i in range(4):
            last(hi, i)

    joint_rows()

    for hi in range(2):
        for own, count in ((True, 3), (False, 4)):

            @pl.when((side == hi) == own)
            def _(hi=hi, count=count):
                wait_bytes(looked.at[pl.ds(0, count)], rb_.at[2 + hi])

    for half in range(2):
        wait_bytes(recv1.at[half, pl.ds(0, NR - 1)], s1.at[half])
    for hi, half in ((0, 0), (1, 0), (1, 1)):
        wait_bytes(recv2.at[hi, half, pl.ds(0, NR - 1)], s2.at[hi, half])
    for j in range(3):
        wait_bytes(recvw.at[pl.ds(0, NB - 1)], sb.at[j])
    kept.wait()


def finish(res, looked, pbf, res_out, ret_out, ret_v, osem):
    outs = [pltpu.make_async_copy(res, res_out, osem.at[2])]
    outs[0].start()
    for hi in range(2):
        for four in range(4):
            seen = looked[2 * four + hi].astype(F32)
            for h in range(2):
                rows, cols = pl.ds(32 * hi + 8 * four, 8), pl.ds(1024 * h, 1024)
                ret_v[rows, cols] = pbf[rows, cols] * seen[8 * h : 8 * h + 8]
        rows = pl.ds(32 * hi, 32)
        outs.append(pltpu.make_async_copy(ret_v.at[rows], ret_out.at[rows], osem.at[hi]))
        outs[1 + hi].start()
    for c in outs:
        c.wait()


def body(dirty, model, psf_spectrum, primary_beam, offsets):
    consts = [jnp.asarray(v) for v in tables()]
    psf = jnp.swapaxes(psf_spectrum[0], 1, 2).reshape(128, N)
    hbm = pl.BlockSpec(memory_space=pl.ANY)
    vmem = pl.BlockSpec(memory_space=pltpu.VMEM)
    image = lambda dt: pltpu.VMEM((ROWS, N), dt)
    rows_in = lambda: pltpu.VMEM((2, NR, 2, 16, 128), BF16)
    rows_out = lambda: pltpu.VMEM((2, 2, NR, 16, 128), BF16)
    beam = lambda: pltpu.VMEM((NB, 16, 1024), BF16)
    scratch = [
        image(BF16), image(F32), image(BF16), pltpu.VMEM((128, N), F32),
        *[pltpu.VMEM(v.shape, v.dtype) for v in consts], pltpu.SMEM((NB,), jnp.int32),
        pltpu.VMEM((2, 256, 512), BF16), rows_in(), rows_in(), rows_out(), rows_out(),
        pltpu.VMEM((4, 2, 256, 128), F32), pltpu.VMEM((32, 64, 128), F32), pltpu.VMEM((2, 2, 128, 512), F32),
        pltpu.VMEM((4, 256, 256), BF16),
        beam(), beam(), beam(), beam(), beam(),
        pltpu.VMEM((NB, 48, 8, 128), F32), pltpu.VMEM((32, 8, 128), F32), pltpu.VMEM((32, 8, 128), F32),
        pltpu.SemaphoreType.DMA((14,)), pltpu.SemaphoreType.DMA,
        pltpu.SemaphoreType.DMA((2,)), pltpu.SemaphoreType.DMA((2,)),
        pltpu.SemaphoreType.DMA((2, 2)), pltpu.SemaphoreType.DMA((2, 2)),
        pltpu.SemaphoreType.DMA((3,)), pltpu.SemaphoreType.DMA((4,)),
    ]
    kept = pl.pallas_call(
        kernel,
        out_shape=[pltpu.VMEM((ROWS, N), F32), pltpu.VMEM((NB, 16, 1024), BF16), pltpu.VMEM((ROWS, N), F32)],
        in_specs=[hbm] * 14,
        out_specs=[vmem] * 3,
        scratch_shapes=scratch,
        compiler_params=pltpu.CompilerParams(
            collective_id=0, has_side_effects=True, vmem_limit_bytes=56 * 1024 * 1024
        ),
    )(model[0], dirty[0], primary_beam[0], psf, offsets, *consts)
    residual, returned = pl.pallas_call(
        finish,
        out_shape=[jax.ShapeDtypeStruct((ROWS, N), F32)] * 2,
        in_specs=[vmem] * 3,
        out_specs=[hbm] * 2,
        scratch_shapes=[image(F32), pltpu.SemaphoreType.DMA((3,))],
        compiler_params=pltpu.CompilerParams(vmem_limit_bytes=56 * 1024 * 1024),
    )(*[pltpu.with_memory_space_constraint(v, pltpu.VMEM) for v in kept])
    return (residual[None], returned[None])


def solution(mesh):
    in_specs = (
        P("beam", "row", None),
        P("beam", "row", None),
        P("beam", None, None, "row"),
        P("beam", "row", None),
        P(),
    )
    out_specs = (P("beam", "row", None), P("beam", "row", None))
    return jax.shard_map(body, mesh=mesh, in_specs=in_specs, out_specs=out_specs, check_vma=False)
```

```python
import math

import jax
import jax.numpy as jnp
import numpy as np
from jax import lax
from jax.experimental import pallas as pl
from jax.experimental.pallas import tpu as pltpu
from jax.sharding import PartitionSpec as P

MESH = pl.DeviceIdType.MESH
F32 = jnp.float32
BF16 = jnp.bfloat16

N = 2048
ROWS = 64
NR = 32
NB = 8
FIRST = (0, 2, 1, 3)
FLOOR = 0.05
FIRST_DONE = (0, 8, 1, 24)
AHEAD, REST = 1, 2
RT = math.sqrt(0.5)


def place(a):
    return 8 * (a % 4) + a // 4


def tables():
    q = np.arange(256)
    k1 = np.arange(8)
    th = 2 * np.pi * (q[None, :] * k1[:, None] % 2048) / 2048
    tw1 = np.stack([np.cos(th), -np.sin(th)]) / math.sqrt(8.0)
    th = 2 * np.pi * (q[:, None] * q[None, :] % 256) / 256
    cos, sin = np.cos(th) / 16, np.sin(th) / 16
    w1 = np.empty((32, 2, 8, 2, 256))
    c3, s3 = cos.reshape(32, 8, 256), sin.reshape(32, 8, 256)
    w1[:, 0, :, 0], w1[:, 0, :, 1] = c3, s3
    w1[:, 1, :, 0], w1[:, 1, :, 1] = -s3, c3
    w4 = np.empty((32, 2, 8, 2, 256))
    w4[:, 0, :, 0], w4[:, 0, :, 1] = c3, s3
    w4[:, 1, :, 0], w4[:, 1, :, 1] = -s3, c3
    r = np.arange(64)
    th = 2 * np.pi * (r[:, None] * r[None, :] % 64) / 64
    cos, sin = np.cos(th) / 8, np.sin(th) / 8
    w2 = np.zeros((2, 2, 64, 2, 2, 64))
    w3 = np.zeros((2, 2, 2, 64, 2, 2, 2, 2, 32))
    for x in range(2):
        w2[0, x, :, 0, x], w2[0, x, :, 1, x] = cos, -sin
        w2[1, x, :, 0, x], w2[1, x, :, 1, x] = sin, cos
        for t in range(2):
            for hi in range(2):
                part = slice(32 * hi, 32 * hi + 32)
                w3[t, 0, x, :, hi, 0, t, x], w3[t, 0, x, :, hi, 1, t, x] = cos[:, part], sin[:, part]
                w3[t, 1, x, :, hi, 0, t, x], w3[t, 1, x, :, hi, 1, t, x] = -sin[:, part], cos[:, part]
    a = np.arange(32)
    th = 2 * np.pi * (r[None, :] * a[:, None] % 2048) / 2048
    tw2 = np.empty((2, 32, 128))
    where = place(a)
    tw2[0, where] = np.tile(np.cos(th), (1, 2)) / math.sqrt(32.0)
    tw2[1, where] = np.tile(-np.sin(th), (1, 2)) / math.sqrt(32.0)
    tw3 = np.empty((2, 2, 32, 128))
    for hi in range(2):
        part = th[:, 32 * hi : 32 * hi + 32]
        tw3[hi, 0, where] = np.tile(np.cos(part), (1, 4)) / math.sqrt(32.0)
        tw3[hi, 1, where] = np.tile(np.sin(part), (1, 4)) / math.sqrt(32.0)
    p1 = np.zeros((256, 256))
    for m in range(8):
        p1[where * 8 + m, 32 * m + a] = 1
    p2 = np.zeros((2, 2, 4, 8, 2, 64))
    for c in range(2):
        for x in range(2):
            for t in range(4):
                for k in range(8):
                    p2[c, x, t, k, c, FIRST[t] + 4 * x + 8 * k] = 1
    bf = lambda v, *s: np.asarray(v.reshape(s), jnp.bfloat16)
    return (
        bf(w1, 512, 512),
        bf(w2, 256, 256),
        bf(w3, 512, 512),
        bf(w4, 512, 512),
        bf(p1, 256, 256),
        bf(p2, 128, 128),
        np.asarray(tw1, np.float32),
        np.asarray(tw2, np.float32),
        np.asarray(tw3, np.float32),
    )


def add(x, y):
    return (x[0] + y[0], x[1] + y[1])


def sub(x, y):
    return (x[0] - y[0], x[1] - y[1])


def turn(x, s):
    return (-x[1], x[0]) if s > 0 else (x[1], -x[0])


def mul(x, c, d):
    return (x[0] * c - x[1] * d, x[0] * d + x[1] * c)


def mul_const(x, num, den, s):
    num %= den
    if num == 0:
        return x
    if 4 * num == den:
        return turn(x, s)
    if 2 * num == den:
        return (-x[0], -x[1])
    if 8 * num == den:
        r = F32(RT)
        return ((x[0] - s * x[1]) * r, (x[1] + s * x[0]) * r)
    if 8 * num == 3 * den:
        r = F32(RT)
        return ((-x[0] - s * x[1]) * r, (s * x[0] - x[1]) * r)
    th = 2 * math.pi * num / den
    return mul(x, F32(math.cos(th)), F32(s * math.sin(th)))


def dft4(x, s):
    t0, t1, t2, t3 = add(x[0], x[2]), sub(x[0], x[2]), add(x[1], x[3]), turn(sub(x[1], x[3]), s)
    return [add(t0, t2), add(t1, t3), sub(t0, t2), sub(t1, t3)]


def dft8(x, s):
    e, o = dft4(x[0::2], s), dft4(x[1::2], s)
    o = [mul_const(o[k], k, 8, s) for k in range(4)]
    return [add(e[k], o[k]) for k in range(4)] + [sub(e[k], o[k]) for k in range(4)]


def dft32_forward(x):
    cols = [dft4([x[8 * p1 + p0] for p1 in range(4)], -1) for p0 in range(8)]
    out = []
    for a0 in range(4):
        out += dft8([mul_const(cols[p0][a0], p0 * a0, 32, -1) for p0 in range(8)], -1)
    return out


def dft32_inverse(x):
    rows = [dft8(x[8 * a0 : 8 * a0 + 8], 1) for a0 in range(4)]
    out = [None] * 32
    for p0 in range(8):
        y = dft4([mul_const(rows[a0][p0], p0 * a0, 32, 1) for a0 in range(4)], 1)
        for p1 in range(4):
            out[8 * p1 + p0] = y[p1]
    return out


def dot(x, y, dims):
    return lax.dot_general(x, y, (dims, ((), ())), preferred_element_type=F32)


NN = ((1,), (0,))
NT = ((1,), (1,))


def kernel(
    model, dirty, pb, psf, offs_h, w1h, w2h, w3h, w4h, p1h, p2h, tw1h, tw2h, tw3h,
    res_v, looked, pbf,
    model_v, dirty_v, pb_v, psf_v, w1, w2, w3, w4, p1, p2, tw1, tw2, tw3, offs,
    z1, send1, recv1, send2, recv2, psfp, y_v, u_v, z2,
    sendw, recvw, send3, recv3, send4, buf, rden, joint,
    lsem, osem, s1, r1, s2, r2, sb, rb_,
):
    bme = lax.axis_index("beam")
    rme = lax.axis_index("row")
    yme, zme = lax.div(rme, 8), lax.rem(rme, 8)
    pair, side = lax.div(bme, 2), lax.rem(bme, 2)

    def row_peer(i):
        dy, dz = (2, 1, 3, 0)[i // 8], (4, 3, 5, 2, 6, 1, 7, 0)[i % 8]
        return lax.rem(yme + dy, 4) * 8 + lax.rem(zme + dz, 8)

    def beam_peer(i):
        chip = lax.rem(pair + (2, 2, 1, 1, 3, 3, 0, 0)[i], 4)
        return 2 * chip + lax.rem(side + (1 + i) % 2, 2)

    def first_row(b):
        return pl.multiple_of(32 * lax.rem(b, 2) + 8 * lax.div(b, 2), 8)

    loads = [
        (model, model_v), (w1h, w1), (tw1h, tw1), (pb, pb_v), (psf, psf_v), (p1h, p1), (p2h, p2),
        (w2h, w2), (w3h, w3), (tw2h, tw2), (w4h, w4), (dirty, dirty_v), (tw3h, tw3), (offs_h, offs),
    ]
    copies = [pltpu.make_async_copy(h, v, lsem.at[i]) for i, (h, v) in enumerate(loads)]
    for c in copies[:3]:
        c.start()

    barrier = pltpu.get_barrier_semaphore()

    for i in range(NR - 1):
        pl.semaphore_signal(barrier, inc=1, device_id=(bme, row_peer(i)), device_id_type=MESH)
    for i in range(NB - 1):
        pl.semaphore_signal(barrier, inc=1, device_id=(beam_peer(i), rme), device_id_type=MESH)
    for c in copies[3:]:
        c.start()

    def send_rows(src, dst, ssem, rsem, part=None):
        def send(peer):
            pltpu.make_async_remote_copy(
                src_ref=src.at[peer],
                dst_ref=dst.at[rme],
                send_sem=ssem,
                recv_sem=rsem,
                device_id=(bme, peer),
                device_id_type=MESH,
            ).start()

        if part == AHEAD:
            for peer in FIRST_DONE:
                pl.when(rme != peer)(lambda peer=peer: send(peer))
        if part != AHEAD:
            for i in range(NR - 1):
                peer = row_peer(i)
                if part == REST:
                    other = peer != FIRST_DONE[0]
                    for one in FIRST_DONE[1:]:
                        other &= peer != one
                    pl.when(other)(lambda peer=peer: send(peer))
                else:
                    send(peer)
            dst[rme] = src[rme]

    def wait_bytes(part, sem):
        pltpu.make_async_copy(part, part, sem).wait()

    def send_beam(peer, src, dst, ssem, rsem):
        pltpu.make_async_remote_copy(
            src_ref=src,
            dst_ref=dst,
            send_sem=ssem,
            recv_sem=rsem,
            device_id=(peer, rme),
            device_id_type=MESH,
        ).start()

    copies[0].wait()
    copies[1].wait()
    copies[2].wait()
    for half in range(2):
        for rb in range(4):
            for qt in range(2):
                rows = pl.ds(16 * rb, 16)
                x = [model_v[rows, pl.ds(256 * p + 128 * qt, 128)].astype(F32) for p in range(8)]
                if half == 0:
                    s04, s26, s15, s37 = x[0] + x[4], x[2] + x[6], x[1] + x[5], x[3] + x[7]
                    e0, o0 = s04 + s26, s15 + s37
                    y2 = (s04 - s26, s37 - s15)
                    y = {0: (e0 + o0, None), 2: y2, 4: (e0 - o0, None), 6: (y2[0], -y2[1])}
                else:
                    a, b, c, d = x[1] - x[5], x[3] - x[7], x[0] - x[4], x[2] - x[6]
                    u, v = (a - b) * F32(RT), (a + b) * F32(RT)
                    y1, y3 = (c + u, -d - v), (c - u, d - v)
                    y = {1: y1, 3: y3, 5: (y3[0], -y3[1]), 7: (y1[0], -y1[1])}
                for k, (re, im) in y.items():
                    tc = tw1[0, pl.ds(k, 1), pl.ds(128 * qt, 128)]
                    ts = tw1[1, pl.ds(k, 1), pl.ds(128 * qt, 128)]
                    if im is None:
                        zr, zi = re * tc, re * ts
                    else:
                        zr, zi = re * tc - im * ts, re * ts + im * tc
                    to = pl.ds(128 * (FIRST.index(k % 4) % 2) + 64 * (k // 4) + 16 * rb, 16)
                    z1[half, to, pl.ds(128 * qt, 128)] = zr.astype(BF16)
                    z1[half, to, pl.ds(256 + 128 * qt, 128)] = zi.astype(BF16)
        out = dot(w1[...], z1[half], NT).astype(BF16)
        for i in range(2):
            send1[half, :, i] = out[:, 128 * i : 128 * i + 128].reshape(NR, 16, 128)
        if half == 0:
            pl.semaphore_wait(barrier, NR - 1 + NB - 1)
        send_rows(send1.at[half], recv1.at[half], s1.at[half], r1.at[half])

    copies[3].wait()
    for g in range(4):
        both = pb_v[pl.ds(16 * g, 16), :].astype(F32)
        pbf[pl.ds(16 * g, 16), :] = both
        for j in range(2):
            part = both[8 * j : 8 * j + 8]
            to = 2 * ((2 * g + j) % 4) + (2 * g + j) // 4
            sendw[to] = jnp.concatenate([part[:, :1024], part[:, 1024:]], axis=0).astype(BF16)

    for i in range(NB - 1):
        peer = beam_peer(i)
        send_beam(peer, sendw.at[peer], recvw.at[bme], sb.at[0], rb_.at[0])
    recvw[bme] = sendw[bme]

    copies[4].wait()
    copies[5].wait()
    copies[6].wait()
    for m in range(8):
        part = psf_v[:, pl.ds(256 * m, 256)].astype(BF16)
        y_v[:, pl.ds(8 * m, 8), :] = dot(p1[...], part, NT).reshape(32, 8, 128)
    low = lax.broadcasted_iota(jnp.int32, (32, 128), 1) < 64
    for a in range(0, 32, 2):
        two = y_v[pl.ds(a, 2)].reshape(128, 128).astype(BF16)
        got = dot(p2[...], two, NT)
        for c in range(2):
            one, two = got[64 * c : 64 * c + 32], got[64 * c + 32 : 64 * c + 64]
            first = jnp.where(low, one, pltpu.roll(two, 64, 1))
            second = jnp.where(low, pltpu.roll(one, 64, 1), two)
            for t in range(4):
                psfp[t, c, pl.ds(8 * a, 8), :] = first[8 * t : 8 * t + 8]
                psfp[t, c, pl.ds(8 * a + 8, 8), :] = second[8 * t : 8 * t + 8]

    for b in range(NB):
        buf[b, pl.ds(0, 16)] = jnp.zeros((16, 8, 128), F32)
        buf[b, pl.ds(32, 16)] = jnp.zeros((16, 8, 128), F32)

    copies[7].wait()
    copies[8].wait()
    copies[9].wait()
    copies[12].wait()
    copies[13].wait()

    def forward_columns(half, i):
        t = 2 * half + i
        x = []
        for p in range(NR):
            both = recv1[half, p, i].astype(F32)
            x.append((both[:8], both[8:]))
        x = dft32_forward(x)
        for a in range(0, NR, 2):
            turned = [mul(x[a + j], tw2[0, pl.ds(a + j, 1), :], tw2[1, pl.ds(a + j, 1), :]) for j in range(2)]
            for c in range(2):
                z2[t, pl.ds(8 * a, 16), pl.ds(128 * c, 128)] = jnp.concatenate(
                    [turned[0][c], turned[1][c]], axis=0
                ).astype(BF16)
        f = dot(z2[t], w2[...], NN)
        fr, fi = f[:, :128], f[:, 128:]
        pr, pi = psfp[t, 0], psfp[t, 1]
        return [(fr * pr - fi * pi).astype(BF16), (fr * pi + fi * pr).astype(BF16)]

    def inverse_columns(h, half, hi):
        g = dot(h, w3[:, pl.ds(256 * hi, 256)], NN)
        x = []
        for a in range(NR):
            gr, gi = g[8 * a : 8 * a + 8, :128], g[8 * a : 8 * a + 8, 128:]
            x.append(mul((gr, gi), tw3[hi, 0, pl.ds(a, 1), :], tw3[hi, 1, pl.ds(a, 1), :]))
        x = dft32_inverse(x)
        for p in range(NR):
            send2[hi, half, p] = jnp.concatenate([x[p][0], x[p][1]], axis=0).astype(BF16)

    def send_back(half, hi, part=None):
        send_rows(send2.at[hi, half], recv2.at[hi, half], s2.at[hi, half], r2.at[hi, half], part)

    for half in range(2):
        wait_bytes(recv1.at[half, pl.ds(0, NR - 1)], r1.at[half])
        h = jnp.concatenate(forward_columns(half, 0) + forward_columns(half, 1), axis=1)
        if half == 0:
            for hi in range(2):
                inverse_columns(h, half, hi)
                send_back(half, hi)
        else:
            for hi in range(2):
                inverse_columns(h, half, hi)
                send_back(half, hi, AHEAD)
            send_back(1, 0, REST)
            wait_bytes(recv2.at[0, 1, pl.ds(0, NR - 1)], s2.at[0, 1])
            send_back(1, 1, REST)

    starts = [16 - offs[b] for b in range(NB)]

    def tile_sum(t):
        ones = [buf[b, starts[b] + t] for b in range(NB)]
        while len(ones) > 1:
            ones = [ones[k] + ones[k + 1] for k in range(0, len(ones), 2)]
        return ones[0]

    wait_bytes(recvw.at[pl.ds(0, NB - 1)], rb_.at[0])
    for b in range(NB):
        for c in range(8):
            both = recvw[b, :, pl.ds(128 * c, 128)].astype(F32)
            both = both * both
            buf[b, 16 + c] = both[:8]
            buf[b, 24 + c] = both[8:]

    def weigh(t, _):
        rden[t] = 1.0 / jnp.maximum(tile_sum(t), FLOOR)
        return 0

    lax.fori_loop(0, 32, weigh, 0)

    def last(hi, i):
        four = lax.rem(pair + (2, 1, 3, 0)[i], 4)
        owner = 2 * four + hi
        row0 = first_row(owner)
        rows = pl.ds(row0, 8)
        for qt in range(2):
            v = []
            for k in range(8):
                t = FIRST.index(k % 4)
                at = pl.ds(pl.multiple_of(64 * (t % 2) + 32 * (k // 4) + 8 * four, 8), 8)
                ur = u_v[hi, t // 2, at, pl.ds(128 * qt, 128)]
                ui = u_v[hi, t // 2, at, pl.ds(256 + 128 * qt, 128)]
                tc = tw1[0, pl.ds(k, 1), pl.ds(128 * qt, 128)]
                ts = -tw1[1, pl.ds(k, 1), pl.ds(128 * qt, 128)]
                re = ur * tc - ui * ts
                v.append((re, None if k % 4 == 0 else ur * ts + ui * tc))
            s = [None] + [(v[k][0] + v[8 - k][0], v[k][1] - v[8 - k][1]) for k in (1, 2, 3)]
            pp, mm = v[0][0] + v[4][0], v[0][0] - v[4][0]
            e1, e2 = pp + s[2][0], pp - s[2][0]
            o1, o2 = mm - s[2][1], mm + s[2][1]
            f, g = s[1][0] + s[3][0], s[1][1] - s[3][1]
            u = F32(RT) * ((s[1][0] - s[1][1]) - (s[3][0] + s[3][1]))
            w = F32(RT) * ((s[1][0] + s[1][1]) - (s[3][0] - s[3][1]))
            conv = [e1 + f, o1 + u, e2 - g, o2 - w, e1 - f, o1 - u, e2 + g, o2 + w]
            weighted = []
            for p in range(8):
                cols = pl.ds(256 * p + 128 * qt, 128)
                one = dirty_v[rows, cols] - conv[p]
                res_v[rows, cols] = one
                weighted.append(pbf[rows, cols] * one)
            for p in range(4):
                send3[owner, :, pl.ds(256 * p + 128 * qt, 128)] = jnp.concatenate(
                    [weighted[p], weighted[p + 4]], axis=0
                ).astype(BF16)

        @pl.when(owner != bme)
        def _():
            send_beam(owner, send3.at[owner], recv3.at[bme], sb.at[1], rb_.at[1])

    kept = pltpu.make_async_copy(send4.at[bme], looked.at[bme], osem)

    def joint_rows():
        recv3[bme] = send3[bme]
        wait_bytes(recv3.at[pl.ds(0, NB - 1)], rb_.at[1])
        for b in range(NB):
            for c in range(8):
                both = recv3[b, :, pl.ds(128 * c, 128)].astype(F32)
                buf[b, 16 + c] = both[:8]
                buf[b, 24 + c] = both[8:]

        for t in range(32):
            joint[t] = tile_sum(t) * rden[t]
        for i in range(NB):
            b = beam_peer(i)
            off = offs[b]
            for c in range(8):
                send4[b, :, pl.ds(128 * c, 128)] = jnp.concatenate(
                    [joint[off + c], joint[off + 8 + c]], axis=0
                ).astype(BF16)
            if i < NB - 1:
                send_beam(b, send4.at[b], looked.at[bme], sb.at[2], rb_.at[2 + side])
        kept.start()

    copies[10].wait()
    copies[11].wait()
    for hi in range(2):
        for half in range(2):
            wait_bytes(recv2.at[hi, half, pl.ds(0, NR - 1)], r2.at[hi, half])
            u_v[hi, half] = dot(recv2[hi, half].reshape(512, 128).T, w4[...], NN)

        for i in range(4):
            last(hi, i)

    joint_rows()

    for hi in range(2):
        for own, count in ((True, 3), (False, 4)):

            @pl.when((side == hi) == own)
            def _(hi=hi, count=count):
                wait_bytes(looked.at[pl.ds(0, count)], rb_.at[2 + hi])

    for half in range(2):
        wait_bytes(recv1.at[half, pl.ds(0, NR - 1)], s1.at[half])
    for hi, half in ((0, 0), (1, 0), (1, 1)):
        wait_bytes(recv2.at[hi, half, pl.ds(0, NR - 1)], s2.at[hi, half])
    for j in range(3):
        wait_bytes(recvw.at[pl.ds(0, NB - 1)], sb.at[j])
    kept.wait()


def finish(res, looked, pbf, res_out, ret_out, ret_v, osem):
    outs = [pltpu.make_async_copy(res, res_out, osem.at[2])]
    outs[0].start()
    for hi in range(2):
        for four in range(4):
            seen = looked[2 * four + hi].astype(F32)
            for h in range(2):
                rows, cols = pl.ds(32 * hi + 8 * four, 8), pl.ds(1024 * h, 1024)
                ret_v[rows, cols] = pbf[rows, cols] * seen[8 * h : 8 * h + 8]
        rows = pl.ds(32 * hi, 32)
        outs.append(pltpu.make_async_copy(ret_v.at[rows], ret_out.at[rows], osem.at[hi]))
        outs[1 + hi].start()
    for c in outs:
        c.wait()


def body(dirty, model, psf_spectrum, primary_beam, offsets):
    consts = [jnp.asarray(v) for v in tables()]
    psf = jnp.swapaxes(psf_spectrum[0], 1, 2).reshape(128, N)
    hbm = pl.BlockSpec(memory_space=pl.ANY)
    vmem = pl.BlockSpec(memory_space=pltpu.VMEM)
    image = lambda dt: pltpu.VMEM((ROWS, N), dt)
    rows_in = lambda: pltpu.VMEM((2, NR, 2, 16, 128), BF16)
    rows_out = lambda: pltpu.VMEM((2, 2, NR, 16, 128), BF16)
    beam = lambda: pltpu.VMEM((NB, 16, 1024), BF16)
    scratch = [
        image(BF16), image(F32), image(BF16), pltpu.VMEM((128, N), F32),
        *[pltpu.VMEM(v.shape, v.dtype) for v in consts], pltpu.SMEM((NB,), jnp.int32),
        pltpu.VMEM((2, 256, 512), BF16), rows_in(), rows_in(), rows_out(), rows_out(),
        pltpu.VMEM((4, 2, 256, 128), F32), pltpu.VMEM((32, 64, 128), F32), pltpu.VMEM((2, 2, 128, 512), F32),
        pltpu.VMEM((4, 256, 256), BF16),
        beam(), beam(), beam(), beam(), beam(),
        pltpu.VMEM((NB, 48, 8, 128), F32), pltpu.VMEM((32, 8, 128), F32), pltpu.VMEM((32, 8, 128), F32),
        pltpu.SemaphoreType.DMA((14,)), pltpu.SemaphoreType.DMA,
        pltpu.SemaphoreType.DMA((2,)), pltpu.SemaphoreType.DMA((2,)),
        pltpu.SemaphoreType.DMA((2, 2)), pltpu.SemaphoreType.DMA((2, 2)),
        pltpu.SemaphoreType.DMA((3,)), pltpu.SemaphoreType.DMA((4,)),
    ]
    kept = pl.pallas_call(
        kernel,
        out_shape=[pltpu.VMEM((ROWS, N), F32), pltpu.VMEM((NB, 16, 1024), BF16), pltpu.VMEM((ROWS, N), F32)],
        in_specs=[hbm] * 14,
        out_specs=[vmem] * 3,
        scratch_shapes=scratch,
        compiler_params=pltpu.CompilerParams(
            collective_id=0, has_side_effects=True, vmem_limit_bytes=56 * 1024 * 1024
        ),
    )(model[0], dirty[0], primary_beam[0], psf, offsets, *consts)
    residual, returned = pl.pallas_call(
        finish,
        out_shape=[jax.ShapeDtypeStruct((ROWS, N), F32)] * 2,
        in_specs=[vmem] * 3,
        out_specs=[hbm] * 2,
        scratch_shapes=[image(F32), pltpu.SemaphoreType.DMA((3,))],
        compiler_params=pltpu.CompilerParams(vmem_limit_bytes=56 * 1024 * 1024),
    )(*[pltpu.with_memory_space_constraint(v, pltpu.VMEM) for v in kept])
    return (residual[None], returned[None])


def solution(mesh):
    in_specs = (
        P("beam", "row", None),
        P("beam", "row", None),
        P("beam", None, None, "row"),
        P("beam", "row", None),
        P(),
    )
    out_specs = (P("beam", "row", None), P("beam", "row", None))
    return jax.shard_map(body, mesh=mesh, in_specs=in_specs, out_specs=out_specs, check_vma=False)
```

```python
import math

import jax
import jax.numpy as jnp
import numpy as np
from jax import lax
from jax.experimental import pallas as pl
from jax.experimental.pallas import tpu as pltpu
from jax.sharding import PartitionSpec as P

MESH = pl.DeviceIdType.MESH
F32 = jnp.float32
BF16 = jnp.bfloat16

N = 2048
ROWS = 64
NR = 32
NB = 8
FIRST = (0, 2, 1, 3)
FLOOR = 0.05
FIRST_DONE = (0, 8, 1, 24)
AHEAD, REST = 1, 2
RT = math.sqrt(0.5)


def place(a):
    return 8 * (a % 4) + a // 4


def tables():
    q = np.arange(256)
    k1 = np.arange(8)
    th = 2 * np.pi * (q[None, :] * k1[:, None] % 2048) / 2048
    tw1 = np.stack([np.cos(th), -np.sin(th)]) / math.sqrt(8.0)
    th = 2 * np.pi * (q[:, None] * q[None, :] % 256) / 256
    cos, sin = np.cos(th) / 16, np.sin(th) / 16
    w1 = np.empty((32, 2, 8, 2, 256))
    c3, s3 = cos.reshape(32, 8, 256), sin.reshape(32, 8, 256)
    w1[:, 0, :, 0], w1[:, 0, :, 1] = c3, s3
    w1[:, 1, :, 0], w1[:, 1, :, 1] = -s3, c3
    w4 = np.empty((32, 2, 8, 2, 256))
    w4[:, 0, :, 0], w4[:, 0, :, 1] = c3, s3
    w4[:, 1, :, 0], w4[:, 1, :, 1] = -s3, c3
    r = np.arange(64)
    th = 2 * np.pi * (r[:, None] * r[None, :] % 64) / 64
    cos, sin = np.cos(th) / 8, np.sin(th) / 8
    w2 = np.zeros((2, 2, 64, 2, 2, 64))
    w3 = np.zeros((2, 2, 2, 64, 2, 2, 2, 2, 32))
    for x in range(2):
        w2[0, x, :, 0, x], w2[0, x, :, 1, x] = cos, -sin
        w2[1, x, :, 0, x], w2[1, x, :, 1, x] = sin, cos
        for t in range(2):
            for hi in range(2):
                part = slice(32 * hi, 32 * hi + 32)
                w3[t, 0, x, :, hi, 0, t, x], w3[t, 0, x, :, hi, 1, t, x] = cos[:, part], sin[:, part]
                w3[t, 1, x, :, hi, 0, t, x], w3[t, 1, x, :, hi, 1, t, x] = -sin[:, part], cos[:, part]
    a = np.arange(32)
    th = 2 * np.pi * (r[None, :] * a[:, None] % 2048) / 2048
    tw2 = np.empty((2, 32, 128))
    where = place(a)
    tw2[0, where] = np.tile(np.cos(th), (1, 2)) / math.sqrt(32.0)
    tw2[1, where] = np.tile(-np.sin(th), (1, 2)) / math.sqrt(32.0)
    tw3 = np.empty((2, 2, 32, 128))
    for hi in range(2):
        part = th[:, 32 * hi : 32 * hi + 32]
        tw3[hi, 0, where] = np.tile(np.cos(part), (1, 4)) / math.sqrt(32.0)
        tw3[hi, 1, where] = np.tile(np.sin(part), (1, 4)) / math.sqrt(32.0)
    p1 = np.zeros((256, 256))
    for m in range(8):
        p1[where * 8 + m, 32 * m + a] = 1
    p2 = np.zeros((2, 2, 4, 8, 2, 64))
    for c in range(2):
        for x in range(2):
            for t in range(4):
                for k in range(8):
                    p2[c, x, t, k, c, FIRST[t] + 4 * x + 8 * k] = 1
    bf = lambda v, *s: np.asarray(v.reshape(s), jnp.bfloat16)
    return (
        bf(w1, 512, 512),
        bf(w2, 256, 256),
        bf(w3, 512, 512),
        bf(w4, 512, 512),
        bf(p1, 256, 256),
        bf(p2, 128, 128),
        np.asarray(tw1, np.float32),
        np.asarray(tw2, np.float32),
        np.asarray(tw3, np.float32),
    )


def add(x, y):
    return (x[0] + y[0], x[1] + y[1])


def sub(x, y):
    return (x[0] - y[0], x[1] - y[1])


def turn(x, s):
    return (-x[1], x[0]) if s > 0 else (x[1], -x[0])


def mul(x, c, d):
    return (x[0] * c - x[1] * d, x[0] * d + x[1] * c)


def mul_const(x, num, den, s):
    num %= den
    if num == 0:
        return x
    if 4 * num == den:
        return turn(x, s)
    if 2 * num == den:
        return (-x[0], -x[1])
    if 8 * num == den:
        r = F32(RT)
        return ((x[0] - s * x[1]) * r, (x[1] + s * x[0]) * r)
    if 8 * num == 3 * den:
        r = F32(RT)
        return ((-x[0] - s * x[1]) * r, (s * x[0] - x[1]) * r)
    th = 2 * math.pi * num / den
    return mul(x, F32(math.cos(th)), F32(s * math.sin(th)))


def dft4(x, s):
    t0, t1, t2, t3 = add(x[0], x[2]), sub(x[0], x[2]), add(x[1], x[3]), turn(sub(x[1], x[3]), s)
    return [add(t0, t2), add(t1, t3), sub(t0, t2), sub(t1, t3)]


def dft8(x, s):
    e, o = dft4(x[0::2], s), dft4(x[1::2], s)
    o = [mul_const(o[k], k, 8, s) for k in range(4)]
    return [add(e[k], o[k]) for k in range(4)] + [sub(e[k], o[k]) for k in range(4)]


def dft32_forward(x):
    cols = [dft4([x[8 * p1 + p0] for p1 in range(4)], -1) for p0 in range(8)]
    out = []
    for a0 in range(4):
        out += dft8([mul_const(cols[p0][a0], p0 * a0, 32, -1) for p0 in range(8)], -1)
    return out


def dft32_inverse(x):
    rows = [dft8(x[8 * a0 : 8 * a0 + 8], 1) for a0 in range(4)]
    out = [None] * 32
    for p0 in range(8):
        y = dft4([mul_const(rows[a0][p0], p0 * a0, 32, 1) for a0 in range(4)], 1)
        for p1 in range(4):
            out[8 * p1 + p0] = y[p1]
    return out


def dot(x, y, dims):
    return lax.dot_general(x, y, (dims, ((), ())), preferred_element_type=F32)


NN = ((1,), (0,))
NT = ((1,), (1,))


def kernel(
    model, dirty, pb, psf, offs_h, w1h, w2h, w3h, w4h, p1h, p2h, tw1h, tw2h, tw3h,
    res_v, looked, pbf,
    model_v, dirty_v, pb_v, psf_v, w1, w2, w3, w4, p1, p2, tw1, tw2, tw3, offs,
    z1, send1, recv1, send2, recv2, psfp, y_v, u_v, z2,
    sendw, recvw, send3, recv3, send4, buf, rden, joint,
    lsem, osem, s1, r1, s2, r2, sb, rb_,
):
    bme = lax.axis_index("beam")
    rme = lax.axis_index("row")
    yme, zme = lax.div(rme, 8), lax.rem(rme, 8)
    pair, side = lax.div(bme, 2), lax.rem(bme, 2)

    def row_peer(i):
        dy, dz = (2, 1, 3, 0)[i // 8], (4, 3, 5, 2, 6, 1, 7, 0)[i % 8]
        return lax.rem(yme + dy, 4) * 8 + lax.rem(zme + dz, 8)

    def beam_peer(i):
        chip = lax.rem(pair + (2, 2, 1, 1, 3, 3, 0, 0)[i], 4)
        return 2 * chip + lax.rem(side + (1 + i) % 2, 2)

    def first_row(b):
        return pl.multiple_of(32 * lax.rem(b, 2) + 8 * lax.div(b, 2), 8)

    loads = [
        (model, model_v), (w1h, w1), (tw1h, tw1), (pb, pb_v), (psf, psf_v), (p1h, p1), (p2h, p2),
        (w2h, w2), (w3h, w3), (tw2h, tw2), (w4h, w4), (dirty, dirty_v), (tw3h, tw3), (offs_h, offs),
    ]
    copies = [pltpu.make_async_copy(h, v, lsem.at[i]) for i, (h, v) in enumerate(loads)]
    for c in copies[:3]:
        c.start()

    barrier = pltpu.get_barrier_semaphore()

    for i in range(NR - 1):
        pl.semaphore_signal(barrier, inc=1, device_id=(bme, row_peer(i)), device_id_type=MESH)
    for i in range(NB - 1):
        pl.semaphore_signal(barrier, inc=1, device_id=(beam_peer(i), rme), device_id_type=MESH)
    for c in copies[3:]:
        c.start()

    def send_rows(src, dst, ssem, rsem, part=None, ahead=()):
        def send(peer):
            pltpu.make_async_remote_copy(
                src_ref=src.at[peer],
                dst_ref=dst.at[rme],
                send_sem=ssem,
                recv_sem=rsem,
                device_id=(bme, peer),
                device_id_type=MESH,
            ).start()

        if part == AHEAD:
            for peer in ahead:
                pl.when(rme != peer)(lambda peer=peer: send(peer))
        if part != AHEAD:
            for i in range(NR - 1):
                peer = row_peer(i)
                if part == REST:
                    other = peer != FIRST_DONE[0]
                    for one in FIRST_DONE[1:]:
                        other &= peer != one
                    pl.when(other)(lambda peer=peer: send(peer))
                else:
                    send(peer)
            dst[rme] = src[rme]

    def wait_bytes(part, sem):
        pltpu.make_async_copy(part, part, sem).wait()

    def send_beam(peer, src, dst, ssem, rsem):
        pltpu.make_async_remote_copy(
            src_ref=src,
            dst_ref=dst,
            send_sem=ssem,
            recv_sem=rsem,
            device_id=(peer, rme),
            device_id_type=MESH,
        ).start()

    copies[0].wait()
    copies[1].wait()
    copies[2].wait()
    for half in range(2):
        for rb in range(4):
            for qt in range(2):
                rows = pl.ds(16 * rb, 16)
                x = [model_v[rows, pl.ds(256 * p + 128 * qt, 128)].astype(F32) for p in range(8)]
                if half == 0:
                    s04, s26, s15, s37 = x[0] + x[4], x[2] + x[6], x[1] + x[5], x[3] + x[7]
                    e0, o0 = s04 + s26, s15 + s37
                    y2 = (s04 - s26, s37 - s15)
                    y = {0: (e0 + o0, None), 2: y2, 4: (e0 - o0, None), 6: (y2[0], -y2[1])}
                else:
                    a, b, c, d = x[1] - x[5], x[3] - x[7], x[0] - x[4], x[2] - x[6]
                    u, v = (a - b) * F32(RT), (a + b) * F32(RT)
                    y1, y3 = (c + u, -d - v), (c - u, d - v)
                    y = {1: y1, 3: y3, 5: (y3[0], -y3[1]), 7: (y1[0], -y1[1])}
                for k, (re, im) in y.items():
                    tc = tw1[0, pl.ds(k, 1), pl.ds(128 * qt, 128)]
                    ts = tw1[1, pl.ds(k, 1), pl.ds(128 * qt, 128)]
                    if im is None:
                        zr, zi = re * tc, re * ts
                    else:
                        zr, zi = re * tc - im * ts, re * ts + im * tc
                    to = pl.ds(128 * (FIRST.index(k % 4) % 2) + 64 * (k // 4) + 16 * rb, 16)
                    z1[half, to, pl.ds(128 * qt, 128)] = zr.astype(BF16)
                    z1[half, to, pl.ds(256 + 128 * qt, 128)] = zi.astype(BF16)
        out = dot(w1[...], z1[half], NT).astype(BF16)
        for i in range(2):
            send1[half, :, i] = out[:, 128 * i : 128 * i + 128].reshape(NR, 16, 128)
        if half == 0:
            pl.semaphore_wait(barrier, NR - 1 + NB - 1)
        send_rows(send1.at[half], recv1.at[half], s1.at[half], r1.at[half])

    copies[3].wait()
    for g in range(4):
        both = pb_v[pl.ds(16 * g, 16), :].astype(F32)
        pbf[pl.ds(16 * g, 16), :] = both
        for j in range(2):
            part = both[8 * j : 8 * j + 8]
            to = 2 * ((2 * g + j) % 4) + (2 * g + j) // 4
            sendw[to] = jnp.concatenate([part[:, :1024], part[:, 1024:]], axis=0).astype(BF16)

    for i in range(NB - 1):
        peer = beam_peer(i)
        send_beam(peer, sendw.at[peer], recvw.at[bme], sb.at[0], rb_.at[0])
    recvw[bme] = sendw[bme]

    copies[4].wait()
    copies[5].wait()
    copies[6].wait()
    for m in range(8):
        part = psf_v[:, pl.ds(256 * m, 256)].astype(BF16)
        y_v[:, pl.ds(8 * m, 8), :] = dot(p1[...], part, NT).reshape(32, 8, 128)
    low = lax.broadcasted_iota(jnp.int32, (32, 128), 1) < 64
    for a in range(0, 32, 2):
        two = y_v[pl.ds(a, 2)].reshape(128, 128).astype(BF16)
        got = dot(p2[...], two, NT)
        for c in range(2):
            one, two = got[64 * c : 64 * c + 32], got[64 * c + 32 : 64 * c + 64]
            first = jnp.where(low, one, pltpu.roll(two, 64, 1))
            second = jnp.where(low, pltpu.roll(one, 64, 1), two)
            for t in range(4):
                psfp[t, c, pl.ds(8 * a, 8), :] = first[8 * t : 8 * t + 8]
                psfp[t, c, pl.ds(8 * a + 8, 8), :] = second[8 * t : 8 * t + 8]

    for b in range(NB):
        buf[b, pl.ds(0, 16)] = jnp.zeros((16, 8, 128), F32)
        buf[b, pl.ds(32, 16)] = jnp.zeros((16, 8, 128), F32)

    copies[7].wait()
    copies[8].wait()
    copies[9].wait()
    copies[12].wait()
    copies[13].wait()

    def forward_columns(half, i):
        t = 2 * half + i
        x = []
        for p in range(NR):
            both = recv1[half, p, i].astype(F32)
            x.append((both[:8], both[8:]))
        x = dft32_forward(x)
        for a in range(0, NR, 2):
            turned = [mul(x[a + j], tw2[0, pl.ds(a + j, 1), :], tw2[1, pl.ds(a + j, 1), :]) for j in range(2)]
            for c in range(2):
                z2[t, pl.ds(8 * a, 16), pl.ds(128 * c, 128)] = jnp.concatenate(
                    [turned[0][c], turned[1][c]], axis=0
                ).astype(BF16)
        f = dot(z2[t], w2[...], NN)
        fr, fi = f[:, :128], f[:, 128:]
        pr, pi = psfp[t, 0], psfp[t, 1]
        return [(fr * pr - fi * pi).astype(BF16), (fr * pi + fi * pr).astype(BF16)]

    def inverse_columns(h, half, hi):
        g = dot(h, w3[:, pl.ds(256 * hi, 256)], NN)
        x = []
        for a in range(NR):
            gr, gi = g[8 * a : 8 * a + 8, :128], g[8 * a : 8 * a + 8, 128:]
            x.append(mul((gr, gi), tw3[hi, 0, pl.ds(a, 1), :], tw3[hi, 1, pl.ds(a, 1), :]))
        x = dft32_inverse(x)
        for p in range(NR):
            send2[hi, half, p] = jnp.concatenate([x[p][0], x[p][1]], axis=0).astype(BF16)

    def send_back(half, hi, part=None, ahead=()):
        send_rows(send2.at[hi, half], recv2.at[hi, half], s2.at[hi, half], r2.at[hi, half], part, ahead)

    starts = [16 - offs[b] for b in range(NB)]

    def tile_sum(t):
        ones = [buf[b, starts[b] + t] for b in range(NB)]
        while len(ones) > 1:
            ones = [ones[k] + ones[k + 1] for k in range(0, len(ones), 2)]
        return ones[0]

    def weigh_all():
        wait_bytes(recvw.at[pl.ds(0, NB - 1)], rb_.at[0])
        for b in range(NB):
            for c in range(8):
                both = recvw[b, :, pl.ds(128 * c, 128)].astype(F32)
                both = both * both
                buf[b, 16 + c] = both[:8]
                buf[b, 24 + c] = both[8:]

        def weigh(t, _):
            rden[t] = 1.0 / jnp.maximum(tile_sum(t), FLOOR)
            return 0

        lax.fori_loop(0, 32, weigh, 0)

    for half in range(2):
        wait_bytes(recv1.at[half, pl.ds(0, NR - 1)], r1.at[half])
        h = jnp.concatenate(forward_columns(half, 0) + forward_columns(half, 1), axis=1)
        if half == 0:
            for hi in range(2):
                inverse_columns(h, half, hi)
                send_back(half, hi)
            weigh_all()
        else:
            for hi in range(2):
                inverse_columns(h, half, hi)
            for peer in FIRST_DONE:
                for hi in range(2):
                    send_back(1, hi, AHEAD, (peer,))
            send_back(1, 0, REST)
            wait_bytes(recv2.at[0, 1, pl.ds(0, NR - 1)], s2.at[0, 1])
            send_back(1, 1, REST)

    def last(hi, i):
        four = lax.rem(pair + (2, 1, 3, 0)[i], 4)
        owner = 2 * four + hi
        row0 = first_row(owner)
        rows = pl.ds(row0, 8)
        for qt in range(2):
            v = []
            for k in range(8):
                t = FIRST.index(k % 4)
                at = pl.ds(pl.multiple_of(64 * (t % 2) + 32 * (k // 4) + 8 * four, 8), 8)
                ur = u_v[hi, t // 2, at, pl.ds(128 * qt, 128)]
                ui = u_v[hi, t // 2, at, pl.ds(256 + 128 * qt, 128)]
                tc = tw1[0, pl.ds(k, 1), pl.ds(128 * qt, 128)]
                ts = -tw1[1, pl.ds(k, 1), pl.ds(128 * qt, 128)]
                re = ur * tc - ui * ts
                v.append((re, None if k % 4 == 0 else ur * ts + ui * tc))
            s = [None] + [(v[k][0] + v[8 - k][0], v[k][1] - v[8 - k][1]) for k in (1, 2, 3)]
            pp, mm = v[0][0] + v[4][0], v[0][0] - v[4][0]
            e1, e2 = pp + s[2][0], pp - s[2][0]
            o1, o2 = mm - s[2][1], mm + s[2][1]
            f, g = s[1][0] + s[3][0], s[1][1] - s[3][1]
            u = F32(RT) * ((s[1][0] - s[1][1]) - (s[3][0] + s[3][1]))
            w = F32(RT) * ((s[1][0] + s[1][1]) - (s[3][0] - s[3][1]))
            conv = [e1 + f, o1 + u, e2 - g, o2 - w, e1 - f, o1 - u, e2 + g, o2 + w]
            weighted = []
            for p in range(8):
                cols = pl.ds(256 * p + 128 * qt, 128)
                one = dirty_v[rows, cols] - conv[p]
                res_v[rows, cols] = one
                weighted.append(pbf[rows, cols] * one)
            for p in range(4):
                send3[owner, :, pl.ds(256 * p + 128 * qt, 128)] = jnp.concatenate(
                    [weighted[p], weighted[p + 4]], axis=0
                ).astype(BF16)

        @pl.when(owner != bme)
        def _():
            send_beam(owner, send3.at[owner], recv3.at[bme], sb.at[1], rb_.at[1])

    kept = pltpu.make_async_copy(send4.at[bme], looked.at[bme], osem)

    def joint_rows():
        recv3[bme] = send3[bme]
        wait_bytes(recv3.at[pl.ds(0, NB - 1)], rb_.at[1])
        for b in range(NB):
            for c in range(8):
                both = recv3[b, :, pl.ds(128 * c, 128)].astype(F32)
                buf[b, 16 + c] = both[:8]
                buf[b, 24 + c] = both[8:]

        for t in range(32):
            joint[t] = tile_sum(t) * rden[t]
        for i in range(NB):
            b = beam_peer(i)
            off = offs[b]
            for c in range(8):
                send4[b, :, pl.ds(128 * c, 128)] = jnp.concatenate(
                    [joint[off + c], joint[off + 8 + c]], axis=0
                ).astype(BF16)
            if i < NB - 1:
                send_beam(b, send4.at[b], looked.at[bme], sb.at[2], rb_.at[2 + side])
        kept.start()

    copies[10].wait()
    copies[11].wait()
    for hi in range(2):
        for half in range(2):
            wait_bytes(recv2.at[hi, half, pl.ds(0, NR - 1)], r2.at[hi, half])
            u_v[hi, half] = dot(recv2[hi, half].reshape(512, 128).T, w4[...], NN)

        for i in range(4):
            last(hi, i)

    joint_rows()

    for hi in range(2):
        for own, count in ((True, 3), (False, 4)):

            @pl.when((side == hi) == own)
            def _(hi=hi, count=count):
                wait_bytes(looked.at[pl.ds(0, count)], rb_.at[2 + hi])

    for half in range(2):
        wait_bytes(recv1.at[half, pl.ds(0, NR - 1)], s1.at[half])
    for hi, half in ((0, 0), (1, 0), (1, 1)):
        wait_bytes(recv2.at[hi, half, pl.ds(0, NR - 1)], s2.at[hi, half])
    for j in range(3):
        wait_bytes(recvw.at[pl.ds(0, NB - 1)], sb.at[j])
    kept.wait()


def finish(res, looked, pbf, res_out, ret_out, ret_v, osem):
    outs = [pltpu.make_async_copy(res, res_out, osem.at[2])]
    outs[0].start()
    for hi in range(2):
        for four in range(4):
            seen = looked[2 * four + hi].astype(F32)
            for h in range(2):
                rows, cols = pl.ds(32 * hi + 8 * four, 8), pl.ds(1024 * h, 1024)
                ret_v[rows, cols] = pbf[rows, cols] * seen[8 * h : 8 * h + 8]
        rows = pl.ds(32 * hi, 32)
        outs.append(pltpu.make_async_copy(ret_v.at[rows], ret_out.at[rows], osem.at[hi]))
        outs[1 + hi].start()
    for c in outs:
        c.wait()


def body(dirty, model, psf_spectrum, primary_beam, offsets):
    consts = [jnp.asarray(v) for v in tables()]
    psf = jnp.swapaxes(psf_spectrum[0], 1, 2).reshape(128, N)
    hbm = pl.BlockSpec(memory_space=pl.ANY)
    vmem = pl.BlockSpec(memory_space=pltpu.VMEM)
    image = lambda dt: pltpu.VMEM((ROWS, N), dt)
    rows_in = lambda: pltpu.VMEM((2, NR, 2, 16, 128), BF16)
    rows_out = lambda: pltpu.VMEM((2, 2, NR, 16, 128), BF16)
    beam = lambda: pltpu.VMEM((NB, 16, 1024), BF16)
    scratch = [
        image(BF16), image(F32), image(BF16), pltpu.VMEM((128, N), F32),
        *[pltpu.VMEM(v.shape, v.dtype) for v in consts], pltpu.SMEM((NB,), jnp.int32),
        pltpu.VMEM((2, 256, 512), BF16), rows_in(), rows_in(), rows_out(), rows_out(),
        pltpu.VMEM((4, 2, 256, 128), F32), pltpu.VMEM((32, 64, 128), F32), pltpu.VMEM((2, 2, 128, 512), F32),
        pltpu.VMEM((4, 256, 256), BF16),
        beam(), beam(), beam(), beam(), beam(),
        pltpu.VMEM((NB, 48, 8, 128), F32), pltpu.VMEM((32, 8, 128), F32), pltpu.VMEM((32, 8, 128), F32),
        pltpu.SemaphoreType.DMA((14,)), pltpu.SemaphoreType.DMA,
        pltpu.SemaphoreType.DMA((2,)), pltpu.SemaphoreType.DMA((2,)),
        pltpu.SemaphoreType.DMA((2, 2)), pltpu.SemaphoreType.DMA((2, 2)),
        pltpu.SemaphoreType.DMA((3,)), pltpu.SemaphoreType.DMA((4,)),
    ]
    kept = pl.pallas_call(
        kernel,
        out_shape=[pltpu.VMEM((ROWS, N), F32), pltpu.VMEM((NB, 16, 1024), BF16), pltpu.VMEM((ROWS, N), F32)],
        in_specs=[hbm] * 14,
        out_specs=[vmem] * 3,
        scratch_shapes=scratch,
        compiler_params=pltpu.CompilerParams(
            collective_id=0, has_side_effects=True, vmem_limit_bytes=56 * 1024 * 1024
        ),
    )(model[0], dirty[0], primary_beam[0], psf, offsets, *consts)
    residual, returned = pl.pallas_call(
        finish,
        out_shape=[jax.ShapeDtypeStruct((ROWS, N), F32)] * 2,
        in_specs=[vmem] * 3,
        out_specs=[hbm] * 2,
        scratch_shapes=[image(F32), pltpu.SemaphoreType.DMA((3,))],
        compiler_params=pltpu.CompilerParams(vmem_limit_bytes=56 * 1024 * 1024),
    )(*[pltpu.with_memory_space_constraint(v, pltpu.VMEM) for v in kept])
    return (residual[None], returned[None])


def solution(mesh):
    in_specs = (
        P("beam", "row", None),
        P("beam", "row", None),
        P("beam", None, None, "row"),
        P("beam", "row", None),
        P(),
    )
    out_specs = (P("beam", "row", None), P("beam", "row", None))
    return jax.shard_map(body, mesh=mesh, in_specs=in_specs, out_specs=out_specs, check_vma=False)
```
